32 devices in a mesh: groups: 2 (over y), out: 8 (over z, x), inp: 2 (over core).
Axes of the slice: x: 2, y: 2, z: 4, core: 2. Of those that a mesh axis runs over, the one named last changes fastest.
Arguments:
- grads: bfloat16 [1024, 28672], P('groups', ('inp', 'out')), parts along dimension 0, may hold values from -6 to 6
- basis_out: bfloat16 [28672, 14336], P('inp', 'out'), may hold values from -0.03125 to 0.03125
- acts: bfloat16 [1024, 8192], P('groups', 'out'), parts along dimension 0, may hold values from -6 to 6
- basis_in: bfloat16 [8192, 8192], P('out', 'inp'), may hold values from -0.09375 to 0.09375
Outputs:
- correction: float32 [28672, 8192], P(('groups', 'out'), 'inp'), parts along dimension 0
The draws below stay inside these ranges and needn't reach their ends.
There are 2 independent parts, one for each index of `groups`. The reference program is written for one: setup_inputs(seed, part) draws one part's arguments, and reference() takes and returns one part's arrays. A program takes and returns all parts, laid end to end along the dimension named above; an argument that names none is the same for every part. Nothing has to cross between parts.
All inputs are finite; a program needn't handle non-finite values.
Results may differ from the reference program's by a relative error of at most 0.0047.
Values may be sent and summed in bfloat16 or wider, within the bound.
No kernel may reach another device: no remote copies, remote signals or barrier semaphores. Data moves between devices by JAX's collectives and lax.ppermute only.
A program may use at most 256 MiB of HBM per device.

```python
import jax
import jax.numpy as jnp

FOUT = 28672
FIN = 8192
EOUT = 14336
TOKENS = 512


def strengthened(values, key, source, target, parts, factor):
    def block_of(axis_at):
        return (jnp.arange(values.shape[axis_at]) // (values.shape[axis_at] // parts)).reshape((-1,) + (1,) * (values.ndim - 1 - axis_at))

    near = jax.random.permutation(key, parts)[block_of(target)]
    other_side = (block_of(target) + parts // 2) % parts
    return jnp.where((block_of(source) == near) | (block_of(source) == other_side), factor * values, values)


def steps_of(rng, extent, pieces, least, top_value):
    def one(position, shards_of):
        draws = jax.random.uniform(jax.random.fold_in(jax.random.fold_in(rng, 6), position), (shards_of,), jnp.float32, least / len(pieces), top_value / len(pieces))
        return jnp.repeat(jnp.exp(draws), extent[position] // shards_of).reshape((-1,) + (1,) * (len(extent) - position - 1))

    factor_of = one(*pieces[0])
    for cut in pieces[1:]:
        factor_of = factor_of * one(*cut)
    return factor_of


def gaussian(rng, dims, scale, reach, shards=(), kind=jnp.bfloat16):
    array = jax.random.normal(rng, dims, jnp.float32) * scale
    if len(shards) > 0:
        array = steps_of(rng, dims, shards, -0.22, 0.18) * array
    return jnp.clip(array, min=-reach, max=reach).astype(kind)


def bell_draw_with(key, extent, width, limit, split, heavy, dtype=jnp.bfloat16):
    values = width * jax.random.normal(key, extent, jnp.float32)
    if split:
        values = values * steps_of(key, extent, split, -0.22, 0.18)
    return jnp.clip(strengthened(values, jax.random.fold_in(key, 3), *heavy), -limit, limit).astype(dtype)


def setup_inputs(seed: int = 0, part: int = 0) -> dict:
    splits = jax.random.split(jax.random.key(seed), 5)
    part_keys = jax.random.split(jax.random.fold_in(splits[4], part), 5)
    grads = gaussian(part_keys[0], (TOKENS, FOUT), 1.0, 6.0, ((1, 16),))
    basis_out = gaussian(splits[1], (FOUT, EOUT), FOUT ** -0.5, 0.03125, ((0, 2), (1, 8)))
    acts = gaussian(part_keys[2], (TOKENS, FIN), 1.0, 6.0, ((1, 8),))
    basis_in = bell_draw_with(splits[3], (FIN, FIN), FIN ** -0.5, 0.09375, ((0, 8), (1, 2)), (0, 1, 8, 2.0))
    return dict(grads=grads, basis_out=basis_out, acts=acts, basis_in=basis_in)


def reference(grads, basis_out, acts, basis_in):
    rot_grad = jnp.dot(grads, basis_out, preferred_element_type=jnp.float32).astype(jnp.bfloat16)
    rot_act = jnp.dot(acts, basis_in, preferred_element_type=jnp.float32).astype(jnp.bfloat16)
    tile = jnp.dot(rot_grad.T, rot_act, preferred_element_type=jnp.float32)
    return tile * tile / jnp.float32(TOKENS)
```

```python
import functools

import jax
import jax.numpy as jnp
from jax import lax
from jax.experimental import pallas as pl
from jax.experimental.pallas import tpu as pltpu
from jax.sharding import PartitionSpec as P

F32, BF16 = jnp.float32, jnp.bfloat16
TN = (((0,), (0,)), ((), ()))
VMEM = 44 * 1024 * 1024
CHEAP = pl.CostEstimate(flops=1000, bytes_accessed=1000, transcendentals=0)


def plain(grads, basis_out, acts, basis_in):
    partial_grad = jnp.dot(
        lax.all_gather(grads, "out", axis=1, tiled=True),
        basis_out,
        preferred_element_type=F32,
    )
    rot_grad = lax.psum(partial_grad, "inp").astype(BF16)
    contract = (((0,), (1,)), ((), ()))
    act_full = lax.dot_general(basis_in, acts, contract, preferred_element_type=F32)
    rot_act = lax.psum(act_full, "out").astype(BF16)
    tile = lax.dot_general(rot_grad, rot_act, contract, preferred_element_type=F32)
    return tile * tile / F32(rot_grad.shape[0])


def pairs(fn):
    out = []
    for z in range(4):
        for x in range(2):
            to = fn(z, x)
            if to is not None:
                out.append((z * 2 + x, to[0] * 2 + to[1]))
    return out


def is_end(z):
    return z in (0, 3)


X_ALL = pairs(lambda z, x: (z, 1 - x))
X_END = pairs(lambda z, x: (z, 1 - x) if is_end(z) else None)
X_MID = pairs(lambda z, x: None if is_end(z) else (z, 1 - x))
Z_NEAR = pairs(lambda z, x: (z ^ 1, x))
Z_MID = pairs(lambda z, x: None if is_end(z) else (3 - z, x))
Z_OUT = pairs(lambda z, x: (z ^ 1, x) if is_end(z) else None)
Z_IN = pairs(lambda z, x: None if is_end(z) else (z ^ 1, x))


def send(name, value, way, axis="out"):
    with jax.named_scope(name):
        return lax.ppermute(value, axis, way)


def after(value, *events):
    return lax.optimization_barrier((value, *events))[0]


def act_kernel(place_ref, acts_ref, basis_ref, wide_ref, narrow_ref):
    part = jnp.dot(acts_ref[...], basis_ref[...], preferred_element_type=F32)
    wide_ref[...] = part
    narrow_ref[...] = part.astype(BF16)


def act_parts(columns, acts, basis_in):
    tokens, depth = acts.shape
    width = basis_in.shape[1]
    step = width // len(columns)
    out_spec = pl.BlockSpec((tokens, step), lambda j, p: (0, j))
    return pl.pallas_call(
        act_kernel,
        grid_spec=pltpu.PrefetchScalarGridSpec(
            num_scalar_prefetch=1,
            grid=(len(columns),),
            in_specs=[
                pl.BlockSpec((tokens, depth), lambda j, p: (0, 0)),
                pl.BlockSpec((depth, step), lambda j, p: (0, p[j])),
            ],
            out_specs=[out_spec, out_spec],
        ),
        out_shape=[
            jax.ShapeDtypeStruct((tokens, width), F32),
            jax.ShapeDtypeStruct((tokens, width), BF16),
        ],
        compiler_params=pltpu.CompilerParams(vmem_limit_bytes=VMEM),
        cost_estimate=CHEAP,
        name="act_parts",
    )(jnp.stack(columns).astype(jnp.int32), acts, basis_in)


def grad_kernel(end_cuts, mid_cuts, place_ref, basis_ref, *refs):
    refs, total_ref, out_ref = refs[:-2], refs[-2], refs[-1]

    def add(cuts):
        acc = total_ref[...]
        row = 0
        for n, width in cuts:
            acc = acc + jnp.dot(refs[n][:, :width], basis_ref[row : row + width], preferred_element_type=F32)
            row += width
        out_ref[...] = acc

    pl.when(place_ref[0] == 1)(lambda: add(end_cuts))
    pl.when(place_ref[0] == 0)(lambda: add(mid_cuts))


def grad_pieces(end, at_end, at_mid, place, basis_out, total):
    arrays = []
    cuts = []
    for sources in (at_end, at_mid):
        cuts.append([])
        for array, width in sources:
            known = [n for n, other in enumerate(arrays) if other is array]
            if not known:
                arrays.append(array)
            cuts[-1].append((known[0] if known else len(arrays) - 1, width))
    depth = sum(width for _, width in cuts[0])
    tokens, width = total.shape
    step = width // 2
    out_spec = pl.BlockSpec((tokens, step), lambda j, s: (0, j))
    return pl.pallas_call(
        functools.partial(grad_kernel, *cuts),
        grid_spec=pltpu.PrefetchScalarGridSpec(
            num_scalar_prefetch=1,
            grid=(width // step,),
            in_specs=[pl.BlockSpec((depth, step), lambda j, s: (s[1], j))]
            + [pl.BlockSpec(array.shape, lambda j, s: (0, 0)) for array in arrays]
            + [out_spec],
            out_specs=out_spec,
        ),
        out_shape=jax.ShapeDtypeStruct((tokens, width), F32),
        compiler_params=pltpu.CompilerParams(vmem_limit_bytes=VMEM),
        cost_estimate=CHEAP,
        name="grad_pieces",
    )(jnp.stack([end.astype(jnp.int32), place.astype(jnp.int32)]), basis_out, *arrays, total)


def grad_sum_kernel(has_total, place_ref, *refs):
    out_ref, refs = refs[-1], refs[:-1]
    acc = None
    if has_total:
        acc, refs = refs[-1][...], refs[:-1]
    count = len(refs) // 2
    for block, basis in zip(refs[:count], refs[count:]):
        part = jnp.dot(block[...], basis[...], preferred_element_type=F32)
        acc = part if acc is None else acc + part
    out_ref[...] = acc


def grad_blocks(pieces, places, basis_out, total):
    tokens, depth = pieces[0].shape
    width = basis_out.shape[1]
    step = width // 2
    whole = pl.BlockSpec((tokens, depth), lambda j, s: (0, 0))
    out_spec = pl.BlockSpec((tokens, step), lambda j, s: (0, j))

    def rows_of(n):
        return pl.BlockSpec((depth, step), lambda j, s: (s[n], j))

    totals = [] if total is None else [total]
    return pl.pallas_call(
        functools.partial(grad_sum_kernel, total is not None),
        grid_spec=pltpu.PrefetchScalarGridSpec(
            num_scalar_prefetch=1,
            grid=(width // step,),
            in_specs=[whole] * len(pieces) + [rows_of(n) for n in range(len(pieces))] + [out_spec] * len(totals),
            out_specs=out_spec,
        ),
        out_shape=jax.ShapeDtypeStruct((tokens, width), F32),
        compiler_params=pltpu.CompilerParams(vmem_limit_bytes=VMEM),
        cost_estimate=CHEAP,
        name="grad_blocks",
    )(jnp.stack(places).astype(jnp.int32), *pieces, *[basis_out] * len(pieces), *totals)


def pick_kernel(place_ref, first_ref, second_ref, out_ref):
    @pl.when(place_ref[0] == 1)
    def _():
        out_ref[...] = first_ref[...]

    @pl.when(place_ref[0] == 0)
    def _():
        out_ref[...] = second_ref[...]


def pick(end, first, first_at, second, second_at, width):
    tokens = first.shape[0]
    step = tokens // 4
    return pl.pallas_call(
        pick_kernel,
        grid_spec=pltpu.PrefetchScalarGridSpec(
            num_scalar_prefetch=1,
            grid=(tokens // step,),
            in_specs=[
                pl.BlockSpec((step, width), lambda i, p: (i * p[0], first_at)),
                pl.BlockSpec((step, width), lambda i, p: (i * (1 - p[0]), second_at)),
            ],
            out_specs=pl.BlockSpec((step, width), lambda i, p: (i, 0)),
        ),
        out_shape=jax.ShapeDtypeStruct((tokens, width), first.dtype),
        compiler_params=pltpu.CompilerParams(vmem_limit_bytes=VMEM),
        cost_estimate=CHEAP,
        name="pick",
    )(end.astype(jnp.int32).reshape(1), first, second)


def lay_kernel(spans, place_ref, *refs):
    out_ref = refs[-1]
    j = pl.program_id(0)
    for ref, (flag, start, count) in zip(refs, spans):

        @pl.when((place_ref[0] == flag) & (j >= start) & (j < start + count))
        def _(ref=ref):
            out_ref[...] = ref[...]


def lay(end, at_end, at_mid, unit):
    tokens = at_mid[0][0].shape[0]
    (one, one_at, count), (two, two_at, other) = at_end[0], at_mid[0]
    if len(at_end) == len(at_mid) == 1 and count == other and one_at % count == two_at % count == 0:
        return pick(end, one, one_at // count, two, two_at // count, count * unit)
    spans, arrays, specs = [], [], []
    units = 0
    for flag, sources in ((1, at_end), (0, at_mid)):
        start = 0
        for array, first, count in sources:

            def index(j, p, flag=flag, start=start, first=first, count=count):
                mine = p[0] if flag else 1 - p[0]
                return 0, first + mine * jnp.clip(j - start, 0, count - 1)

            spans.append((flag, start, count))
            arrays.append(array)
            specs.append(pl.BlockSpec((tokens, unit), index))
            start += count
        units = max(units, start)
    return pl.pallas_call(
        functools.partial(lay_kernel, spans),
        grid_spec=pltpu.PrefetchScalarGridSpec(
            num_scalar_prefetch=1,
            grid=(units,),
            in_specs=specs,
            out_specs=pl.BlockSpec((tokens, unit), lambda j, p: (0, j)),
        ),
        out_shape=jax.ShapeDtypeStruct((tokens, units * unit), arrays[0].dtype),
        compiler_params=pltpu.CompilerParams(vmem_limit_bytes=VMEM),
        cost_estimate=CHEAP,
        name="lay",
    )(end.astype(jnp.int32).reshape(1), *arrays)


def sum_kernel(cut, count, place_ref, *refs):
    out_ref, refs = refs[-1], refs[:-1]
    j = pl.program_id(0)

    def add():
        if cut:
            blocks = [jnp.where(j < cut, refs[0][...], refs[1][...])] + [r[...] for r in refs[2 : len(refs) - 1]]
        else:
            blocks = [r[...] for r in refs[:-1]]
        total = blocks[0].astype(F32)
        for block in blocks[1:]:
            total = total + block.astype(F32)
        out_ref[...] = total.astype(out_ref.dtype)

    if count:
        pl.when((place_ref[0] == 1) & (j < count))(lambda: out_ref.__setitem__(..., refs[-1][...]))
        pl.when((place_ref[0] == 0) | (j >= count))(add)
    else:
        add()


def add_parts(end, sources, units, unit, cut=0, rider=None):
    tokens = sources[0][0].shape[0]

    def spec(n, first):
        if cut and n < 2:
            low, high = (0, cut - 1) if n == 0 else (cut, units - 1)
            return pl.BlockSpec((tokens, unit), lambda j, p: (0, first + jnp.clip(j, low, high) - low))
        return pl.BlockSpec((tokens, unit), lambda j, p: (0, first + j))

    array, first, count = rider or (sources[-1][0], sources[-1][1], 0)
    return pl.pallas_call(
        functools.partial(sum_kernel, cut, count),
        grid_spec=pltpu.PrefetchScalarGridSpec(
            num_scalar_prefetch=1,
            grid=(units,),
            in_specs=[spec(n, f) for n, (_, f) in enumerate(sources)]
            + [pl.BlockSpec((tokens, unit), lambda j, p: (0, first + jnp.clip(j, 0, max(count - 1, 0))))],
            out_specs=pl.BlockSpec((tokens, unit), lambda j, p: (0, j)),
        ),
        out_shape=jax.ShapeDtypeStruct((tokens, units * unit), BF16),
        compiler_params=pltpu.CompilerParams(vmem_limit_bytes=VMEM),
        cost_estimate=CHEAP,
        name="add_parts",
    )(end.astype(jnp.int32).reshape(1), *[source for source, _ in sources], array)


def tile_kernel(tokens, place_ref, grad_ref, first_ref, second_ref, *refs):
    def put(act_ref):
        tile = lax.dot_general(grad_ref[...], act_ref[...], TN, preferred_element_type=F32)
        refs[-1][...] = tile * tile / F32(tokens)

    pl.when(pl.program_id(1) == 0)(lambda: put(first_ref))
    pl.when(pl.program_id(1) == 1)(lambda: put(second_ref))


def tile_part(rot_grad, acts, columns, out, shape):
    tokens, rows = rot_grad.shape
    width = acts[0].shape[1]
    step = rows // 2
    outs = [] if out is None else [out]
    return pl.pallas_call(
        functools.partial(tile_kernel, tokens),
        grid_spec=pltpu.PrefetchScalarGridSpec(
            num_scalar_prefetch=1,
            grid=(rows // step, 2),
            in_specs=[pl.BlockSpec((tokens, step), lambda i, j, p: (0, i))]
            + [pl.BlockSpec((tokens, width), lambda i, j, p: (0, 0))] * 2
            + [pl.BlockSpec(memory_space=pl.ANY)] * len(outs),
            out_specs=pl.BlockSpec((step, width), lambda i, j, p: (i, p[j])),
        ),
        out_shape=jax.ShapeDtypeStruct(shape, F32),
        input_output_aliases={4: 0} if outs else {},
        compiler_params=pltpu.CompilerParams(vmem_limit_bytes=VMEM),
        cost_estimate=CHEAP,
        name="tile_part",
    )(jnp.stack(columns).astype(jnp.int32), rot_grad, *acts, *outs)


def barrier(*values):
    return lax.optimization_barrier(values)


def grid_of_eight(grads, basis_out, acts, basis_in):
    o = lax.axis_index("out")
    z, x = o // 2, o % 2
    side = z // 2
    end = (z == 0) | (z == 3)
    near, far, farthest = z ^ 1, 2 - side, 3 - 3 * side
    eighth = basis_in.shape[1] // 8
    half = grads.shape[1] // 2

    def either(at_end, at_mid):
        return jnp.where(end, at_end, at_mid)

    def z_block(zb, xb):
        return zb * 2 + xb

    def column(ds, dx, h):
        return ((side ^ ds) * 2 + (x ^ dx)) * 2 + h

    unit = eighth // 2

    def blocks(pieces, places, total):
        return grad_blocks(pieces, places, basis_out, total)

    def block_of(at_end, at_mid, place, total):
        at_end = [(array, units * unit) for array, units in at_end]
        at_mid = [(array, units * unit) for array, units in at_mid]
        return grad_pieces(end, at_end, at_mid, place, basis_out, total)

    def put(at_end, at_mid):
        return lay(end, at_end, at_mid, unit)

    def summed(sources, units, **more):
        return add_parts(end, sources, units, unit, **more)

    a = send("near", grads, Z_NEAR)
    x0 = send("own_x", grads, X_ALL)
    b1 = send("mid_own", grads, Z_MID)
    order = [(1, 1, 0), (1, 0, 0), (0, 1, 0), (0, 0, 0), (1, 1, 1), (1, 0, 1), (0, 1, 1), (0, 0, 1)]
    wide, narrow = act_parts([column(*e) for e in order], acts, basis_in)
    total = blocks([after(grads, wide)], [z_block(z, x)], None)

    b1, total = barrier(b1, total)
    a, total = barrier(a, total)
    b2 = send("mid_near", a, Z_MID)
    y1 = put([(narrow, 0, 7)], [(b1, 0, 7)])
    r1 = send("r1", y1, Z_NEAR)
    x1 = send("x1", put([(after(a, y1), 0, 7)], [(b1, 0, 7)]), X_ALL)
    total = blocks([a, x0], [z_block(near, x), z_block(z, 1 - x)], total)

    b2, total = barrier(b2, total)
    y2 = put([(narrow, 7, 5)], [(b2, 0, 5)])
    r2_h = send("r2_h", y2, Z_NEAR)
    r1, y2, total = barrier(r1, y2, total)
    y3 = put([(r1, 0, 7)], [(b2, 0, 7)])
    x2 = send("x2", y3, X_ALL)
    y4 = summed([(after(wide, y3), 0), (r1, 0)], 4)
    m_a = send("mid_a", y4, Z_MID)
    y5 = put([(after(narrow, y4), 12, 4)], [(b2, 5, 2)])
    r2_t = send("r2_t", y5, Z_NEAR)
    x1, total = barrier(x1, total)
    total = blocks([x1], [z_block(either(near, far), 1 - x)], after(total, y5))

    r2_h, total = barrier(r2_h, total)
    y6 = summed([(wide, 8), (r2_h, 1)], 4)
    m_b = send("mid_b", y6, Z_MID)
    x3_h = send("x3_h", after(r2_h, y6), X_END)
    m_a, y6, total = barrier(m_a, y6, total)
    y7 = summed([(wide, 4), (r1, 4), (m_a, 0)], 2)
    xm_a = send("sum_x_a", y7, X_MID)
    total = block_of([(r1, 7)], [(b1, 7)], z_block(far, x), after(total, y7))

    x2, total = barrier(x2, total)
    r2_t, total = barrier(r2_t, total)
    xm_a, total = barrier(xm_a, total)
    t00_a = summed([(r1, 6), (r2_h, 0), (wide, 6), (m_a, 2), (xm_a, 0)], 2, cut=1, rider=(x0, 3, 2))
    t10_a = send("all_mid_a", t00_a, Z_MID)
    e00_a = send("all_in_0a", t00_a, Z_NEAR)
    m_b, t00_a = barrier(m_b, t00_a)
    y9 = summed([(after(wide, t00_a), 12), (r2_t, 0), (m_b, 0)], 2)
    xm_b = send("sum_x_b", y9, X_MID)
    total = blocks([x2], [z_block(either(far, farthest), 1 - x)], after(total, y9))

    x3_h, total = barrier(x3_h, total)
    y8 = put([(r2_t, 0, 2)], [(after(a, total), 0, 3)])
    x3_t = send("x3_t", y8, X_ALL)
    t10_a, e00_a, y8 = barrier(t10_a, e00_a, y8)
    y10 = put([(x0, 5, 2)], [(t10_a, 0, 2)])
    e10_a = send("all_in_1a", y10, Z_NEAR)
    u00_a = put([(after(e00_a, y10), 0, 2)], [(t00_a, 0, 2)])
    s01_a = send("all_x_0a", u00_a, X_ALL)
    xm_b, u00_a = barrier(xm_b, u00_a)
    t00_b = summed([(after(wide, u00_a), 14), (r2_t, 2), (m_b, 2), (xm_b, 0)], 2)
    t10_b = send("all_mid_b", t00_b, Z_MID)
    e00_b = send("all_in_0b", t00_b, Z_IN)

    e10_a, t00_b = barrier(e10_a, t00_b)
    u10_a = put([(e10_a, 0, 2)], [(after(t10_a, t00_b), 0, 2)])
    s11_a = send("all_x_1a", u10_a, X_ALL)
    total = block_of([(r2_h, 5), (r2_t, 2)], [(b2, 7)], z_block(farthest, x), after(total, u10_a))
    x3_t, total = barrier(x3_t, total)
    s01_a, total = barrier(s01_a, total)
    total = block_of([(x3_h, 5), (x3_t, 2)], [(x3_t, 3), (e00_a, 2), (e10_a, 2)], z_block(either(farthest, near), 1 - x), total)

    t10_b, e00_b, total = barrier(t10_b, e00_b, total)
    s11_a, total = barrier(s11_a, total)
    other = [send("core", piece, [(0, 1), (1, 0)], "inp") for piece in jnp.split(total, 8)]
    e10_b = send("all_in_1b", t10_b, Z_IN)
    u00_b = put([(e00_b, 0, 2)], [(t00_b, 0, 2)])
    s01_b = send("all_x_0b", u00_b, X_ALL)
    rot_grad = (after(total, u00_b) + jnp.concatenate(other)).astype(BF16)
    shape = (basis_out.shape[1], basis_in.shape[1])

    def tile(parts, dx, h, out):
        return tile_part(rot_grad, parts, [column(0, dx, h), column(1, dx, h)], out, shape)

    out = tile((u00_a, u10_a), 0, 0, None)
    out = tile((s01_a, s11_a), 1, 0, out)
    s01_b, out = barrier(s01_b, out)

    e10_b, out = barrier(e10_b, out)
    u10_b = put([(e10_b, 0, 2)], [(t10_b, 0, 2)])
    s11_b = send("all_x_1b", u10_b, X_ALL)
    out = tile((u00_b, u10_b), 0, 1, out)
    return tile((s01_b, s11_b), 1, 1, out)


def solution(mesh):
    return jax.shard_map(
        grid_of_eight if mesh.shape["out"] == 8 and mesh.shape["inp"] == 2 else plain,
        mesh=mesh,
        in_specs=(
            P("groups", ("inp", "out")),
            P("inp", "out"),
            P("groups", "out"),
            P("out", "inp"),
        ),
        out_specs=P(("groups", "out"), "inp"),
        check_vma=False,
    )
```

```python
import functools

import jax
import jax.numpy as jnp
from jax import lax
from jax.experimental import pallas as pl
from jax.experimental.pallas import tpu as pltpu
from jax.sharding import PartitionSpec as P

F32, BF16 = jnp.float32, jnp.bfloat16
TN = (((0,), (0,)), ((), ()))
VMEM = 44 * 1024 * 1024
CHEAP = pl.CostEstimate(flops=1000, bytes_accessed=1000, transcendentals=0)


def plain(grads, basis_out, acts, basis_in):
    partial_grad = jnp.dot(
        lax.all_gather(grads, "out", axis=1, tiled=True),
        basis_out,
        preferred_element_type=F32,
    )
    rot_grad = lax.psum(partial_grad, "inp").astype(BF16)
    contract = (((0,), (1,)), ((), ()))
    act_full = lax.dot_general(basis_in, acts, contract, preferred_element_type=F32)
    rot_act = lax.psum(act_full, "out").astype(BF16)
    tile = lax.dot_general(rot_grad, rot_act, contract, preferred_element_type=F32)
    return tile * tile / F32(rot_grad.shape[0])


def pairs(fn):
    out = []
    for z in range(4):
        for x in range(2):
            to = fn(z, x)
            if to is not None:
                out.append((z * 2 + x, to[0] * 2 + to[1]))
    return out


def is_end(z):
    return z in (0, 3)


X_ALL = pairs(lambda z, x: (z, 1 - x))
X_END = pairs(lambda z, x: (z, 1 - x) if is_end(z) else None)
X_MID = pairs(lambda z, x: None if is_end(z) else (z, 1 - x))
Z_NEAR = pairs(lambda z, x: (z ^ 1, x))
Z_MID = pairs(lambda z, x: None if is_end(z) else (3 - z, x))
X_END_Z_MID = pairs(lambda z, x: (z, 1 - x) if is_end(z) else (3 - z, x))
Z_IN = pairs(lambda z, x: None if is_end(z) else (z ^ 1, x))


def send(name, value, way, axis="out"):
    with jax.named_scope(name):
        return lax.ppermute(value, axis, way)


def after(value, *events):
    return lax.optimization_barrier((value, *events))[0]


def pinned(*arrays):
    return [pltpu.with_memory_space_constraint(array, pltpu.HBM) for array in arrays]


def act_kernel(spans, place_ref, acts_ref, basis_ref, wide_ref, *narrow_refs):
    part = jnp.dot(acts_ref[...], basis_ref[...], preferred_element_type=F32)
    wide_ref[...] = part
    narrow = part.astype(BF16)
    for j, pieces in enumerate(spans):

        @pl.when(pl.program_id(0) == j)
        def _(pieces=pieces):
            for n, into, first, width in pieces:
                narrow_refs[n][:, into : into + width] = narrow[:, first : first + width]


def act_parts(columns, sent, unit, acts, basis_in):
    tokens, depth = acts.shape
    width = basis_in.shape[1]
    step = 2 * unit
    spans = [[] for _ in columns]
    for n, units in enumerate(sent):
        for at, u in enumerate(units):
            spans[u // 2].append((n, at * unit, (u % 2) * unit, unit))
    return pl.pallas_call(
        functools.partial(act_kernel, spans),
        grid_spec=pltpu.PrefetchScalarGridSpec(
            num_scalar_prefetch=1,
            grid=(len(columns),),
            in_specs=[
                pl.BlockSpec((tokens, depth), lambda j, p: (0, 0)),
                pl.BlockSpec((depth, step), lambda j, p: (0, p[j])),
            ],
            out_specs=[pl.BlockSpec((tokens, step), lambda j, p: (0, j))]
            + [pl.BlockSpec((tokens, len(units) * unit), lambda j, p: (0, 0)) for units in sent],
        ),
        out_shape=[pltpu.HBM((tokens, width), F32)] + [pltpu.HBM((tokens, len(units) * unit), BF16) for units in sent],
        compiler_params=pltpu.CompilerParams(vmem_limit_bytes=VMEM),
        cost_estimate=CHEAP,
        name="act_parts",
    )(jnp.stack(columns).astype(jnp.int32), *pinned(acts, basis_in))


def grad_kernel(end_cuts, mid_cuts, outs, place_ref, basis_ref, *refs):
    refs, total_ref, out_refs = refs[: -outs - 1], refs[-outs - 1], refs[-outs:]

    def add(cuts):
        acc = total_ref[...]
        row = 0
        for n, first, width in cuts:
            piece = refs[n][:, first : first + width]
            acc = acc + jnp.dot(piece, basis_ref[row : row + width], preferred_element_type=F32)
            row += width
        if outs == 1:
            out_refs[0][...] = acc
            return
        for n, out_ref in enumerate(out_refs):

            @pl.when(pl.program_id(0) == n)
            def _(out_ref=out_ref):
                out_ref[...] = acc

    pl.when(place_ref[0] == 1)(lambda: add(end_cuts))
    pl.when(place_ref[0] == 0)(lambda: add(mid_cuts))


def grad_pieces(end, at_end, at_mid, place, basis_out, total, halves=False):
    arrays = []
    cuts = []
    for sources in (at_end, at_mid):
        cuts.append([])
        for array, first, width in sources:
            known = [n for n, other in enumerate(arrays) if other is array]
            if not known:
                arrays.append(array)
            cuts[-1].append((known[0] if known else len(arrays) - 1, first, width))
    depth = sum(width for _, _, width in cuts[0])
    tokens, width = total.shape
    step = width // 2
    out_spec = pl.BlockSpec((tokens, step), lambda j, s: (0, j))
    half_spec = pl.BlockSpec((tokens, step), lambda j, s: (0, 0))
    return pl.pallas_call(
        functools.partial(grad_kernel, *cuts, 2 if halves else 1),
        grid_spec=pltpu.PrefetchScalarGridSpec(
            num_scalar_prefetch=1,
            grid=(2,),
            in_specs=[pl.BlockSpec((depth, step), lambda j, s: (s[1], j))]
            + [pl.BlockSpec(array.shape, lambda j, s: (0, 0)) for array in arrays]
            + [out_spec],
            out_specs=[half_spec] * 2 if halves else out_spec,
        ),
        out_shape=[pltpu.HBM((tokens, step), F32)] * 2 if halves else pltpu.HBM((tokens, width), F32),
        compiler_params=pltpu.CompilerParams(vmem_limit_bytes=VMEM),
        cost_estimate=CHEAP,
        name="grad_pieces",
    )(jnp.stack([end.astype(jnp.int32), place.astype(jnp.int32)]), *pinned(basis_out), *arrays, *pinned(total))


def grad_sum_kernel(has_total, place_ref, *refs):
    out_ref, refs = refs[-1], refs[:-1]
    acc = None
    if has_total:
        acc, refs = refs[-1][...], refs[:-1]
    count = len(refs) // 2
    for block, basis in zip(refs[:count], refs[count:]):
        part = jnp.dot(block[...], basis[...], preferred_element_type=F32)
        acc = part if acc is None else acc + part
    out_ref[...] = acc


def grad_blocks(pieces, places, basis_out, total):
    tokens, depth = pieces[0].shape
    width = basis_out.shape[1]
    step = width // 2 if len(pieces) == 1 else 256
    whole = pl.BlockSpec((tokens, depth), lambda j, s: (0, 0))
    out_spec = pl.BlockSpec((tokens, step), lambda j, s: (0, j))

    def rows_of(n):
        return pl.BlockSpec((depth, step), lambda j, s: (s[n], j))

    totals = [] if total is None else [total]
    return pl.pallas_call(
        functools.partial(grad_sum_kernel, total is not None),
        grid_spec=pltpu.PrefetchScalarGridSpec(
            num_scalar_prefetch=1,
            grid=(width // step,),
            in_specs=[whole] * len(pieces) + [rows_of(n) for n in range(len(pieces))] + [out_spec] * len(totals),
            out_specs=out_spec,
        ),
        out_shape=pltpu.HBM((tokens, width), F32),
        compiler_params=pltpu.CompilerParams(vmem_limit_bytes=VMEM),
        cost_estimate=CHEAP,
        name="grad_blocks",
    )(jnp.stack(places).astype(jnp.int32), *pinned(*pieces, *[basis_out] * len(pieces), *totals))


def make_kernel(plans, place_ref, *refs):
    out_ref = refs[-1]

    def write(layers):
        at = 0
        for columns in layers:
            total = None
            for n, first, width in columns:
                block = refs[n][:, first : first + width]
                if len(columns) > 1:
                    block = block.astype(F32)
                total = block if total is None else total + block
            out_ref[:, at : at + columns[0][2]] = total.astype(out_ref.dtype)
            at += columns[0][2]

    for flag, layers in plans:
        if layers is not None:
            pl.when(place_ref[0] == flag)(lambda layers=layers: write(layers))


def make(end, at_end, at_mid, units, unit):
    arrays, specs, keys, plans = [], [], [], []
    small = units <= 2
    rows = (at_mid or at_end)[0][0][0].shape[0]
    steps = 1 if small else 2
    rows //= steps
    for flag, ranges in ((1, at_end), (0, at_mid)):
        if ranges is None:
            plans.append((flag, None))
            continue
        plan = []
        for sources in ranges:
            columns = []
            for array, first, count in sources:
                aligned = first % count == 0
                width = count * unit if aligned else array.shape[1]
                column = first // count if aligned else 0
                key = (id(array), width, column, flag)
                if key not in keys:
                    keys.append(key)
                    arrays.append(array)
                    specs.append(
                        pl.BlockSpec(
                            (rows, width),
                            lambda i, p, flag=flag, column=column: (i * (p[0] if flag else 1 - p[0]), column),
                        )
                    )
                columns.append((keys.index(key), 0 if aligned else first * unit, count * unit))
            plan.append(columns)
        plans.append((flag, plan))
    return pl.pallas_call(
        functools.partial(make_kernel, plans),
        grid_spec=pltpu.PrefetchScalarGridSpec(
            num_scalar_prefetch=1,
            grid=(steps,),
            in_specs=specs,
            out_specs=pl.BlockSpec((rows, units * unit), lambda i, p: (i, 0)),
        ),
        out_shape=(jax.ShapeDtypeStruct if small else pltpu.HBM)((steps * rows, units * unit), BF16),
        compiler_params=pltpu.CompilerParams(vmem_limit_bytes=VMEM),
        cost_estimate=CHEAP,
        name="make",
    )(end.astype(jnp.int32).reshape(1), *[a if a.shape[1] <= 2 * unit else pinned(a)[0] for a in arrays])


def tile_kernel(tokens, count, place_ref, low_ref, high_ref, *refs):
    out_ref = refs[-1]
    rows = low_ref.shape[1]
    for n in range(count):

        @pl.when(pl.program_id(0) == n)
        def _(n=n):
            for at, grad_ref in ((0, low_ref), (rows, high_ref)):
                tile = lax.dot_general(grad_ref[...], refs[n][...], TN, preferred_element_type=F32)
                out_ref[at : at + rows] = tile * tile / F32(tokens)


def tile_part(rot_grad, acts, columns, out, shape):
    tokens, rows = rot_grad[0].shape
    count = len(acts)
    width = acts[0].shape[1]
    outs = [] if out is None else [out]
    return pl.pallas_call(
        functools.partial(tile_kernel, tokens, count),
        grid_spec=pltpu.PrefetchScalarGridSpec(
            num_scalar_prefetch=1,
            grid=(count,),
            in_specs=[pl.BlockSpec((tokens, rows), lambda j, p: (0, 0))] * 2
            + [pl.BlockSpec((tokens, width), lambda j, p: (0, 0))] * count
            + [pl.BlockSpec(memory_space=pl.ANY)] * len(outs),
            out_specs=pl.BlockSpec((2 * rows, width), lambda j, p: (0, p[j])),
        ),
        out_shape=jax.ShapeDtypeStruct(shape, F32),
        input_output_aliases={3 + count: 0} if outs else {},
        compiler_params=pltpu.CompilerParams(vmem_limit_bytes=VMEM),
        cost_estimate=CHEAP,
        name="tile_part",
    )(jnp.stack(columns).astype(jnp.int32), *rot_grad, *acts, *outs)


def barrier(*values):
    return lax.optimization_barrier(values)


def grid_of_eight(grads, basis_out, acts, basis_in):
    o = lax.axis_index("out")
    z, x = o // 2, o % 2
    side = z // 2
    end = (z == 0) | (z == 3)
    near, far, farthest = z ^ 1, 2 - side, 3 - 3 * side
    eighth = basis_in.shape[1] // 8
    half = grads.shape[1] // 2

    def either(at_end, at_mid):
        return jnp.where(end, at_end, at_mid)

    def z_block(zb, xb):
        return zb * 2 + xb

    def column(ds, dx, h):
        return ((side ^ ds) * 2 + (x ^ dx)) * 2 + h

    unit = eighth // 2

    def blocks(pieces, places, total):
        return grad_blocks(pieces, places, basis_out, total)

    def block_of(at_end, at_mid, place, total, halves=False):
        at_end = [(array, first * unit, units * unit) for array, first, units in at_end]
        at_mid = [(array, first * unit, units * unit) for array, first, units in at_mid]
        return grad_pieces(end, at_end, at_mid, place, basis_out, total, halves)

    def put(at_end, at_mid, units):
        return make(end, at_end, at_mid, units, unit)

    def one(array, first, units):
        return [[(array, first, units)]]

    a = send("near", grads, Z_NEAR)
    x0 = send("own_x", grads, X_ALL)
    b1 = send("mid_own", grads, Z_MID)
    order = [(1, 1, 0), (1, 0, 0), (0, 1, 0), (0, 0, 0), (1, 1, 1), (1, 0, 1), (0, 1, 1), (0, 0, 1)]
    sent = [0, 1, 2, 3, 4, 5, 6], [8, 9, 10, 11, 7], [12, 13, 14, 15]
    wide, n1, n2, n3 = act_parts([column(*e) for e in order], sent, unit, acts, basis_in)
    total = blocks([after(grads, wide)], [z_block(z, x)], None)

    a, total = barrier(a, total)
    c1 = send("near_on", a, X_END_Z_MID)
    b1, total = barrier(b1, total)
    y1 = put(one(n1, 0, 7), one(b1, 0, 7), 7)
    r1 = send("r1", y1, Z_NEAR)
    xb1 = send("mid_own_x", after(b1, y1), X_MID)
    total = blocks([a, x0], [z_block(near, x), z_block(z, 1 - x)], total)

    b2, total = barrier(c1, total)
    y2 = put(one(n2, 0, 5), one(b2, 0, 5), 5)
    r2_h = send("r2_h", y2, Z_NEAR)
    r1, y2, total = barrier(r1, y2, total)
    y3 = put(one(r1, 0, 7), one(b2, 0, 7), 7)
    x2 = send("x2", y3, X_ALL)
    y4 = put(None, [[(after(wide, y3), 0, 4), (r1, 0, 4)]], 4)
    m_a = send("mid_a", y4, Z_MID)
    y5 = put(one(after(n3, y4), 0, 4), one(b2, 5, 2), 4)
    r2_t = send("r2_t", y5, Z_NEAR)
    xb1, total = barrier(xb1, total)
    total = block_of([(b2, 0, 7)], [(xb1, 0, 7)], z_block(either(near, far), 1 - x), after(total, y5))
    total = block_of([(r1, 0, 7)], [(b1, 0, 7)], z_block(far, x), total)

    r2_h, total = barrier(r2_h, total)
    y6 = put(None, [[(wide, 8, 4), (r2_h, 0, 4)]], 4)
    m_b = send("mid_b", y6, Z_MID)
    x3_h = send("x3_h", after(r2_h, y6), X_END)
    m_a, y6, total = barrier(m_a, y6, total)
    y7 = put(None, [[(wide, 4, 2), (r1, 4, 2), (m_a, 0, 2)]], 2)
    xm_a = send("sum_x_a", y7, X_MID)
    x2, total = barrier(x2, after(total, y7))
    total = blocks([x2], [z_block(either(far, farthest), 1 - x)], total)

    r2_t, total = barrier(r2_t, total)
    xm_a, total = barrier(xm_a, total)
    sums = [
        [(r1, 6, 1), (wide, 6, 1), (m_a, 2, 1), (xm_a, 0, 1)],
        [(r2_h, 4, 1), (wide, 7, 1), (m_a, 3, 1), (xm_a, 1, 1)],
    ]
    t00_a = put(one(x0, 2, 2), sums, 2)
    t10_a = send("all_mid_a", t00_a, Z_MID)
    e00_a = send("all_in_0a", t00_a, Z_NEAR)
    m_b, t00_a = barrier(m_b, t00_a)
    y9 = put(None, [[(after(wide, t00_a), 12, 2), (r2_t, 0, 2), (m_b, 0, 2)]], 2)
    xm_b = send("sum_x_b", y9, X_MID)
    y8 = put(one(after(r2_t, y9), 0, 2), [[(a, 0, 2)], [(a, 6, 1)]], 3)

    t10_a, e00_a, y8 = barrier(t10_a, e00_a, y8)
    y10 = put(one(x0, 4, 2), one(t10_a, 0, 2), 2)
    e10_a = send("all_in_1a", y10, Z_NEAR)
    x3_h, y10 = barrier(x3_h, y10)
    x3_t = send("x3_t", after(y8, y10), X_ALL)
    xm_b, y10 = barrier(xm_b, y10)
    sums = [[(after(wide, y10), 14, 2), (r2_t, 2, 2), (m_b, 2, 2), (xm_b, 0, 2)]]
    t00_b = put(None, sums, 2)
    t10_b = send("all_mid_b", t00_b, Z_MID)
    e00_b = send("all_in_0b", t00_b, Z_IN)
    u00_a = put(one(after(e00_a, t00_b), 0, 2), one(t00_a, 0, 2), 2)
    s01_a = send("all_x_0a", u00_a, X_ALL)

    e10_a, u00_a = barrier(e10_a, u00_a)
    u10_a = put(one(e10_a, 0, 2), one(after(t10_a, u00_a), 0, 2), 2)
    s11_a = send("all_x_1a", u10_a, X_ALL)
    total = block_of([(r2_h, 0, 5), (r2_t, 0, 2)], [(b2, 0, 7)], z_block(farthest, x), after(total, u10_a))
    x3_t, total = barrier(x3_t, total)

    t10_b, e00_b, total = barrier(t10_b, e00_b, total)
    e10_b = send("all_in_1b", t10_b, Z_IN)
    u00_b = put(one(e00_b, 0, 2), one(t00_b, 0, 2), 2)
    s01_b = send("all_x_0b", u00_b, X_ALL)
    s01_a, total = barrier(s01_a, after(total, u00_b))
    at_end = [(x3_h, 0, 5), (x3_t, 0, 2)]
    at_mid = [(x3_t, 0, 2), (e00_a, 0, 2), (e10_a, 0, 2), (x3_t, 2, 1)]
    low, high = block_of(at_end, at_mid, z_block(either(farthest, near), 1 - x), total, halves=True)

    s11_a, e10_b, low, high = barrier(s11_a, e10_b, low, high)
    low_other = send("core_low", low, [(0, 1), (1, 0)], "inp")
    high_other = send("core_high", high, [(0, 1), (1, 0)], "inp")
    u10_b = put(one(e10_b, 0, 2), one(t10_b, 0, 2), 2)
    s11_b = send("all_x_1b", u10_b, X_ALL)
    rot_grad = [
        (mine + theirs).astype(BF16) for mine, theirs in ((after(low, u10_b), low_other), (after(high, u10_b), high_other))
    ]
    shape = (basis_out.shape[1], basis_in.shape[1])
    places = [column(0, 0, 0), column(1, 0, 0), column(0, 1, 0), column(1, 1, 0)]
    out = tile_part(rot_grad, [u00_a, u10_a, s01_a, s11_a], places, None, shape)
    s01_b, out = barrier(s01_b, out)
    out = tile_part(rot_grad, [u00_b, u10_b, s01_b], [column(0, 0, 1), column(1, 0, 1), column(0, 1, 1)], out, shape)
    return tile_part(rot_grad, [s11_b], [column(1, 1, 1)], out, shape)


def solution(mesh):
    return jax.shard_map(
        grid_of_eight if mesh.shape["out"] == 8 and mesh.shape["inp"] == 2 else plain,
        mesh=mesh,
        in_specs=(
            P("groups", ("inp", "out")),
            P("inp", "out"),
            P("groups", "out"),
            P("out", "inp"),
        ),
        out_specs=P(("groups", "out"), "inp"),
        check_vma=False,
    )
```

```python
import functools

import jax
import jax.numpy as jnp
from jax import lax
from jax.experimental import pallas as pl
from jax.experimental.pallas import tpu as pltpu
from jax.sharding import PartitionSpec as P

F32, BF16 = jnp.float32, jnp.bfloat16
TN = (((0,), (0,)), ((), ()))
VMEM = 44 * 1024 * 1024
CHEAP = pl.CostEstimate(flops=1000, bytes_accessed=1000, transcendentals=0)


def plain(grads, basis_out, acts, basis_in):
    partial_grad = jnp.dot(
        lax.all_gather(grads, "out", axis=1, tiled=True),
        basis_out,
        preferred_element_type=F32,
    )
    rot_grad = lax.psum(partial_grad, "inp").astype(BF16)
    contract = (((0,), (1,)), ((), ()))
    act_full = lax.dot_general(basis_in, acts, contract, preferred_element_type=F32)
    rot_act = lax.psum(act_full, "out").astype(BF16)
    tile = lax.dot_general(rot_grad, rot_act, contract, preferred_element_type=F32)
    return tile * tile / F32(rot_grad.shape[0])


def pairs(fn):
    out = []
    for z in range(4):
        for x in range(2):
            to = fn(z, x)
            if to is not None:
                out.append((z * 2 + x, to[0] * 2 + to[1]))
    return out


def is_end(z):
    return z in (0, 3)


X_ALL = pairs(lambda z, x: (z, 1 - x))
X_END = pairs(lambda z, x: (z, 1 - x) if is_end(z) else None)
X_MID = pairs(lambda z, x: None if is_end(z) else (z, 1 - x))
Z_NEAR = pairs(lambda z, x: (z ^ 1, x))
Z_MID = pairs(lambda z, x: None if is_end(z) else (3 - z, x))
X_END_Z_MID = pairs(lambda z, x: (z, 1 - x) if is_end(z) else (3 - z, x))
Z_IN = pairs(lambda z, x: None if is_end(z) else (z ^ 1, x))


def send(name, value, way, axis="out"):
    with jax.named_scope(name):
        return lax.ppermute(value, axis, way)


def after(value, *events):
    return lax.optimization_barrier((value, *events))[0]


def pinned(*arrays):
    return [pltpu.with_memory_space_constraint(array, pltpu.HBM) for array in arrays]


def act_kernel(spans, place_ref, acts_ref, basis_ref, wide_ref, *narrow_refs):
    part = jnp.dot(acts_ref[...], basis_ref[...], preferred_element_type=F32)
    wide_ref[...] = part
    narrow = part.astype(BF16)
    for j, pieces in enumerate(spans):

        @pl.when(pl.program_id(0) == j)
        def _(pieces=pieces):
            for n, into, first, width in pieces:
                narrow_refs[n][:, into : into + width] = narrow[:, first : first + width]


def act_parts(columns, sent, unit, acts, basis_in):
    tokens, depth = acts.shape
    width = basis_in.shape[1]
    step = 2 * unit
    spans = [[] for _ in columns]
    for n, units in enumerate(sent):
        for at, u in enumerate(units):
            spans[u // 2].append((n, at * unit, (u % 2) * unit, unit))
    return pl.pallas_call(
        functools.partial(act_kernel, spans),
        grid_spec=pltpu.PrefetchScalarGridSpec(
            num_scalar_prefetch=1,
            grid=(len(columns),),
            in_specs=[
                pl.BlockSpec((tokens, depth), lambda j, p: (0, 0)),
                pl.BlockSpec((depth, step), lambda j, p: (0, p[j])),
            ],
            out_specs=[pl.BlockSpec((tokens, step), lambda j, p: (0, j))]
            + [pl.BlockSpec((tokens, len(units) * unit), lambda j, p: (0, 0)) for units in sent],
        ),
        out_shape=[pltpu.HBM((tokens, width), F32)] + [pltpu.HBM((tokens, len(units) * unit), BF16) for units in sent],
        compiler_params=pltpu.CompilerParams(vmem_limit_bytes=VMEM),
        cost_estimate=CHEAP,
        name="act_parts",
    )(jnp.stack(columns).astype(jnp.int32), *pinned(acts, basis_in))


def grad_kernel(end_cuts, mid_cuts, outs, place_ref, basis_ref, *refs):
    refs, total_ref, out_refs = refs[: -outs - 1], refs[-outs - 1], refs[-outs:]

    def add(cuts):
        acc = total_ref[...]
        row = 0
        for n, first, width in cuts:
            piece = refs[n][:, first : first + width]
            acc = acc + jnp.dot(piece, basis_ref[row : row + width], preferred_element_type=F32)
            row += width
        if outs == 1:
            out_refs[0][...] = acc
            return
        for n, out_ref in enumerate(out_refs):

            @pl.when(pl.program_id(0) == n)
            def _(out_ref=out_ref):
                out_ref[...] = acc

    pl.when(place_ref[0] == 1)(lambda: add(end_cuts))
    pl.when(place_ref[0] == 0)(lambda: add(mid_cuts))


def grad_pieces(end, at_end, at_mid, place, basis_out, total, halves=False):
    arrays = []
    cuts = []
    for sources in (at_end, at_mid):
        cuts.append([])
        for array, first, width in sources:
            known = [n for n, other in enumerate(arrays) if other is array]
            if not known:
                arrays.append(array)
            cuts[-1].append((known[0] if known else len(arrays) - 1, first, width))
    depth = sum(width for _, _, width in cuts[0])
    tokens, width = total.shape
    step = width // 2
    out_spec = pl.BlockSpec((tokens, step), lambda j, s: (0, j))
    half_spec = pl.BlockSpec((tokens, step), lambda j, s: (0, 0))
    return pl.pallas_call(
        functools.partial(grad_kernel, *cuts, 2 if halves else 1),
        grid_spec=pltpu.PrefetchScalarGridSpec(
            num_scalar_prefetch=1,
            grid=(2,),
            in_specs=[pl.BlockSpec((depth, step), lambda j, s: (s[1], j))]
            + [pl.BlockSpec(array.shape, lambda j, s: (0, 0)) for array in arrays]
            + [out_spec],
            out_specs=[half_spec] * 2 if halves else out_spec,
        ),
        out_shape=[pltpu.HBM((tokens, step), F32)] * 2 if halves else pltpu.HBM((tokens, width), F32),
        compiler_params=pltpu.CompilerParams(vmem_limit_bytes=VMEM),
        cost_estimate=CHEAP,
        name="grad_pieces",
    )(jnp.stack([end.astype(jnp.int32), place.astype(jnp.int32)]), *pinned(basis_out), *arrays, *pinned(total))


def grad_sum_kernel(has_total, place_ref, *refs):
    out_ref, refs = refs[-1], refs[:-1]
    acc = None
    if has_total:
        acc, refs = refs[-1][...], refs[:-1]
    count = len(refs) // 2
    for block, basis in zip(refs[:count], refs[count:]):
        part = jnp.dot(block[...], basis[...], preferred_element_type=F32)
        acc = part if acc is None else acc + part
    out_ref[...] = acc


def grad_blocks(pieces, places, basis_out, total):
    tokens, depth = pieces[0].shape
    width = basis_out.shape[1]
    step = width // 2 if len(pieces) == 1 else 256
    whole = pl.BlockSpec((tokens, depth), lambda j, s: (0, 0))
    out_spec = pl.BlockSpec((tokens, step), lambda j, s: (0, j))

    def rows_of(n):
        return pl.BlockSpec((depth, step), lambda j, s: (s[n], j))

    totals = [] if total is None else [total]
    return pl.pallas_call(
        functools.partial(grad_sum_kernel, total is not None),
        grid_spec=pltpu.PrefetchScalarGridSpec(
            num_scalar_prefetch=1,
            grid=(width // step,),
            in_specs=[whole] * len(pieces) + [rows_of(n) for n in range(len(pieces))] + [out_spec] * len(totals),
            out_specs=out_spec,
        ),
        out_shape=pltpu.HBM((tokens, width), F32),
        compiler_params=pltpu.CompilerParams(vmem_limit_bytes=VMEM),
        cost_estimate=CHEAP,
        name="grad_blocks",
    )(jnp.stack(places).astype(jnp.int32), *pinned(*pieces, *[basis_out] * len(pieces), *totals))


def make_kernel(plans, place_ref, *refs):
    out_ref = refs[-1]

    def write(layers):
        at = 0
        for columns in layers:
            total = None
            for n, first, width in columns:
                block = refs[n][:, first : first + width]
                if len(columns) > 1:
                    block = block.astype(F32)
                total = block if total is None else total + block
            out_ref[:, at : at + columns[0][2]] = total.astype(out_ref.dtype)
            at += columns[0][2]

    for flag, layers in plans:
        if layers is not None:
            pl.when(place_ref[0] == flag)(lambda layers=layers: write(layers))


def make(end, at_end, at_mid, units, unit):
    arrays, specs, keys, plans = [], [], [], []
    small = units <= 2
    rows = (at_mid or at_end)[0][0][0].shape[0]
    steps = 1 if small else 2
    rows //= steps
    for flag, ranges in ((1, at_end), (0, at_mid)):
        if ranges is None:
            plans.append((flag, None))
            continue
        plan = []
        for sources in ranges:
            columns = []
            for array, first, count in sources:
                aligned = first % count == 0
                width = count * unit if aligned else array.shape[1]
                column = first // count if aligned else 0
                key = (id(array), width, column, flag)
                if key not in keys:
                    keys.append(key)
                    arrays.append(array)
                    specs.append(
                        pl.BlockSpec(
                            (rows, width),
                            lambda i, p, flag=flag, column=column: (i * (p[0] if flag else 1 - p[0]), column),
                        )
                    )
                columns.append((keys.index(key), 0 if aligned else first * unit, count * unit))
            plan.append(columns)
        plans.append((flag, plan))
    return pl.pallas_call(
        functools.partial(make_kernel, plans),
        grid_spec=pltpu.PrefetchScalarGridSpec(
            num_scalar_prefetch=1,
            grid=(steps,),
            in_specs=specs,
            out_specs=pl.BlockSpec((rows, units * unit), lambda i, p: (i, 0)),
        ),
        out_shape=(jax.ShapeDtypeStruct if small else pltpu.HBM)((steps * rows, units * unit), BF16),
        compiler_params=pltpu.CompilerParams(vmem_limit_bytes=VMEM),
        cost_estimate=CHEAP,
        name="make",
    )(end.astype(jnp.int32).reshape(1), *[a if a.shape[1] <= 2 * unit else pinned(a)[0] for a in arrays])


def tile_kernel(tokens, count, place_ref, low_ref, high_ref, *refs):
    out_ref = refs[-1]
    rows = low_ref.shape[1]
    for n in range(count):

        @pl.when(pl.program_id(0) == n)
        def _(n=n):
            for at, grad_ref in ((0, low_ref), (rows, high_ref)):
                tile = lax.dot_general(grad_ref[...], refs[n][...], TN, preferred_element_type=F32)
                out_ref[at : at + rows] = tile * tile / F32(tokens)


def tile_part(rot_grad, acts, columns, out, shape):
    tokens, rows = rot_grad[0].shape
    count = len(acts)
    width = acts[0].shape[1]
    outs = [] if out is None else [out]
    return pl.pallas_call(
        functools.partial(tile_kernel, tokens, count),
        grid_spec=pltpu.PrefetchScalarGridSpec(
            num_scalar_prefetch=1,
            grid=(count,),
            in_specs=[pl.BlockSpec((tokens, rows), lambda j, p: (0, 0))] * 2
            + [pl.BlockSpec((tokens, width), lambda j, p: (0, 0))] * count
            + [pl.BlockSpec(memory_space=pl.ANY)] * len(outs),
            out_specs=pl.BlockSpec((2 * rows, width), lambda j, p: (0, p[j])),
        ),
        out_shape=jax.ShapeDtypeStruct(shape, F32),
        input_output_aliases={3 + count: 0} if outs else {},
        compiler_params=pltpu.CompilerParams(vmem_limit_bytes=VMEM),
        cost_estimate=CHEAP,
        name="tile_part",
    )(jnp.stack(columns).astype(jnp.int32), *rot_grad, *acts, *outs)


def barrier(*values):
    return lax.optimization_barrier(values)


def grid_of_eight(grads, basis_out, acts, basis_in):
    o = lax.axis_index("out")
    z, x = o // 2, o % 2
    side = z // 2
    end = (z == 0) | (z == 3)
    near, far, farthest = z ^ 1, 2 - side, 3 - 3 * side
    eighth = basis_in.shape[1] // 8
    half = grads.shape[1] // 2

    def either(at_end, at_mid):
        return jnp.where(end, at_end, at_mid)

    def z_block(zb, xb):
        return zb * 2 + xb

    def column(ds, dx, h):
        return ((side ^ ds) * 2 + (x ^ dx)) * 2 + h

    unit = eighth // 2

    def blocks(pieces, places, total):
        return grad_blocks(pieces, places, basis_out, total)

    def block_of(at_end, at_mid, place, total, halves=False):
        at_end = [(array, first * unit, units * unit) for array, first, units in at_end]
        at_mid = [(array, first * unit, units * unit) for array, first, units in at_mid]
        return grad_pieces(end, at_end, at_mid, place, basis_out, total, halves)

    def put(at_end, at_mid, units):
        return make(end, at_end, at_mid, units, unit)

    def one(array, first, units):
        return [[(array, first, units)]]

    a = send("near", grads, Z_NEAR)
    x0 = send("own_x", grads, X_ALL)
    b1 = send("mid_own", grads, Z_MID)
    order = [(1, 1, 0), (1, 0, 0), (0, 1, 0), (0, 0, 0), (1, 1, 1), (1, 0, 1), (0, 1, 1), (0, 0, 1)]
    sent = [0, 1, 2, 3, 4, 5, 6], [8, 9, 10, 11, 7], [12, 13, 14, 15]
    wide, n1, n2, n3 = act_parts([column(*e) for e in order], sent, unit, acts, basis_in)
    total = blocks([after(grads, wide)], [z_block(z, x)], None)

    a, total = barrier(a, total)
    c1 = send("near_on", a, X_END_Z_MID)
    b1, total = barrier(b1, total)
    y1 = put(one(n1, 0, 7), one(b1, 0, 7), 7)
    r1 = send("r1", y1, Z_NEAR)
    xb1 = send("mid_own_x", after(b1, y1), X_MID)
    total = blocks([a, x0], [z_block(near, x), z_block(z, 1 - x)], total)

    b2, total = barrier(c1, total)
    y2 = put(one(n2, 0, 5), one(b2, 0, 5), 5)
    r2_h = send("r2_h", y2, Z_NEAR)
    r1, y2, total = barrier(r1, y2, total)
    y3 = put(one(r1, 0, 7), one(b2, 0, 7), 7)
    x2 = send("x2", y3, X_ALL)
    y4 = put(None, [[(after(wide, y3), 0, 4), (r1, 0, 4)]], 4)
    m_a = send("mid_a", y4, Z_MID)
    y5 = put(one(after(n3, y4), 0, 4), one(b2, 5, 2), 4)
    r2_t = send("r2_t", y5, Z_NEAR)
    xb1, total = barrier(xb1, total)
    total = block_of([(b2, 0, 7)], [(xb1, 0, 7)], z_block(either(near, far), 1 - x), after(total, y5))
    total = block_of([(r1, 0, 7)], [(b1, 0, 7)], z_block(far, x), total)

    r2_h, total = barrier(r2_h, total)
    y6 = put(None, [[(wide, 8, 4), (r2_h, 0, 4)]], 4)
    m_b = send("mid_b", y6, Z_MID)
    x3_h = send("x3_h", after(r2_h, y6), X_END)
    m_a, y6, total = barrier(m_a, y6, total)
    y7 = put(None, [[(wide, 4, 2), (r1, 4, 2), (m_a, 0, 2)]], 2)
    xm_a = send("sum_x_a", y7, X_MID)
    x2, total = barrier(x2, after(total, y7))
    total = blocks([x2], [z_block(either(far, farthest), 1 - x)], total)

    r2_t, total = barrier(r2_t, total)
    xm_a, total = barrier(xm_a, total)
    sums = [
        [(r1, 6, 1), (wide, 6, 1), (m_a, 2, 1), (xm_a, 0, 1)],
        [(r2_h, 4, 1), (wide, 7, 1), (m_a, 3, 1), (xm_a, 1, 1)],
    ]
    t00_a = put(one(x0, 2, 2), sums, 2)
    e00_a = send("all_in_0a", t00_a, Z_NEAR)
    t10_a = send("all_mid_a", t00_a, Z_MID)
    m_b, t00_a = barrier(m_b, t00_a)
    y9 = put(None, [[(after(wide, t00_a), 12, 2), (r2_t, 0, 2), (m_b, 0, 2)]], 2)
    xm_b = send("sum_x_b", y9, X_MID)
    y8 = put(one(after(r2_t, y9), 0, 2), [[(a, 0, 2)], [(a, 6, 1)]], 3)

    e00_a, y8 = barrier(e00_a, y8)
    t10_a, y8 = barrier(t10_a, y8)
    y10 = put(one(x0, 4, 2), one(t10_a, 0, 2), 2)
    e10_a = send("all_in_1a", y10, Z_NEAR)
    x3_h, y10 = barrier(x3_h, y10)
    x3_t = send("x3_t", after(y8, y10), X_ALL)
    xm_b, y10 = barrier(xm_b, y10)
    sums = [[(after(wide, y10), 14, 2), (r2_t, 2, 2), (m_b, 2, 2), (xm_b, 0, 2)]]
    t00_b = put(None, sums, 2)
    t10_b = send("all_mid_b", t00_b, Z_MID)
    e00_b = send("all_in_0b", t00_b, Z_IN)
    u00_a = put(one(after(e00_a, t00_b), 0, 2), one(t00_a, 0, 2), 2)
    s01_a = send("all_x_0a", u00_a, X_ALL)

    e10_a, u00_a = barrier(e10_a, u00_a)
    u10_a = put(one(e10_a, 0, 2), one(after(t10_a, u00_a), 0, 2), 2)
    s11_a = send("all_x_1a", u10_a, X_ALL)
    total = block_of([(r2_h, 0, 5), (r2_t, 0, 2)], [(b2, 0, 7)], z_block(farthest, x), after(total, u10_a))
    x3_t, total = barrier(x3_t, total)

    t10_b, e00_b, total = barrier(t10_b, e00_b, total)
    e10_b = send("all_in_1b", t10_b, Z_IN)
    u00_b = put(one(e00_b, 0, 2), one(t00_b, 0, 2), 2)
    s01_b = send("all_x_0b", u00_b, X_ALL)
    s01_a, total = barrier(s01_a, after(total, u00_b))
    at_end = [(x3_h, 0, 5), (x3_t, 0, 2)]
    at_mid = [(x3_t, 0, 2), (e00_a, 0, 2), (e10_a, 0, 2), (x3_t, 2, 1)]
    low, high = block_of(at_end, at_mid, z_block(either(farthest, near), 1 - x), total, halves=True)

    s11_a, e10_b, low, high = barrier(s11_a, e10_b, low, high)
    low_other = send("core_low", low, [(0, 1), (1, 0)], "inp")
    high_other = send("core_high", high, [(0, 1), (1, 0)], "inp")
    u10_b = put(one(e10_b, 0, 2), one(t10_b, 0, 2), 2)
    s11_b = send("all_x_1b", u10_b, X_ALL)
    rot_grad = [
        (mine + theirs).astype(BF16) for mine, theirs in ((after(low, u10_b), low_other), (after(high, u10_b), high_other))
    ]
    shape = (basis_out.shape[1], basis_in.shape[1])
    places = [column(0, 0, 0), column(1, 0, 0), column(0, 1, 0), column(1, 1, 0)]
    out = tile_part(rot_grad, [u00_a, u10_a, s01_a, s11_a], places, None, shape)
    s01_b, out = barrier(s01_b, out)
    out = tile_part(rot_grad, [u00_b, u10_b, s01_b], [column(0, 0, 1), column(1, 0, 1), column(0, 1, 1)], out, shape)
    return tile_part(rot_grad, [s11_b], [column(1, 1, 1)], out, shape)


def solution(mesh):
    return jax.shard_map(
        grid_of_eight if mesh.shape["out"] == 8 and mesh.shape["inp"] == 2 else plain,
        mesh=mesh,
        in_specs=(
            P("groups", ("inp", "out")),
            P("inp", "out"),
            P("groups", "out"),
            P("out", "inp"),
        ),
        out_specs=P(("groups", "out"), "inp"),
        check_vma=False,
    )
```

```python
import functools

import jax
import jax.numpy as jnp
from jax import lax
from jax.experimental import pallas as pl
from jax.experimental.pallas import tpu as pltpu
from jax.sharding import PartitionSpec as P

F32, BF16 = jnp.float32, jnp.bfloat16
TN = (((0,), (0,)), ((), ()))
VMEM = 44 * 1024 * 1024
CHEAP = pl.CostEstimate(flops=1000, bytes_accessed=1000, transcendentals=0)


def plain(grads, basis_out, acts, basis_in):
    partial_grad = jnp.dot(
        lax.all_gather(grads, "out", axis=1, tiled=True),
        basis_out,
        preferred_element_type=F32,
    )
    rot_grad = lax.psum(partial_grad, "inp").astype(BF16)
    contract = (((0,), (1,)), ((), ()))
    act_full = lax.dot_general(basis_in, acts, contract, preferred_element_type=F32)
    rot_act = lax.psum(act_full, "out").astype(BF16)
    tile = lax.dot_general(rot_grad, rot_act, contract, preferred_element_type=F32)
    return tile * tile / F32(rot_grad.shape[0])


def pairs(fn):
    out = []
    for z in range(4):
        for x in range(2):
            to = fn(z, x)
            if to is not None:
                out.append((z * 2 + x, to[0] * 2 + to[1]))
    return out


def is_end(z):
    return z in (0, 3)


X_ALL = pairs(lambda z, x: (z, 1 - x))
X_END = pairs(lambda z, x: (z, 1 - x) if is_end(z) else None)
X_MID = pairs(lambda z, x: None if is_end(z) else (z, 1 - x))
Z_NEAR = pairs(lambda z, x: (z ^ 1, x))
Z_MID = pairs(lambda z, x: None if is_end(z) else (3 - z, x))
X_END_Z_MID = pairs(lambda z, x: (z, 1 - x) if is_end(z) else (3 - z, x))
Z_IN = pairs(lambda z, x: None if is_end(z) else (z ^ 1, x))


def send(name, value, way, axis="out"):
    with jax.named_scope(name):
        return lax.ppermute(value, axis, way)


def after(value, *events):
    return lax.optimization_barrier((value, *events))[0]


def pinned(*arrays):
    return [pltpu.with_memory_space_constraint(array, pltpu.HBM) for array in arrays]


def act_kernel(spans, place_ref, acts_ref, basis_ref, wide_ref, *narrow_refs):
    part = jnp.dot(acts_ref[...], basis_ref[...], preferred_element_type=F32)
    wide_ref[...] = part
    narrow = part.astype(BF16)
    for j, pieces in enumerate(spans):

        @pl.when(pl.program_id(0) == j)
        def _(pieces=pieces):
            for n, into, first, width in pieces:
                narrow_refs[n][:, into : into + width] = narrow[:, first : first + width]


def act_parts(columns, sent, unit, acts, basis_in):
    tokens, depth = acts.shape
    width = basis_in.shape[1]
    step = 2 * unit
    spans = [[] for _ in columns]
    for n, units in enumerate(sent):
        for at, u in enumerate(units):
            spans[u // 2].append((n, at * unit, (u % 2) * unit, unit))
    return pl.pallas_call(
        functools.partial(act_kernel, spans),
        grid_spec=pltpu.PrefetchScalarGridSpec(
            num_scalar_prefetch=1,
            grid=(len(columns),),
            in_specs=[
                pl.BlockSpec((tokens, depth), lambda j, p: (0, 0)),
                pl.BlockSpec((depth, step), lambda j, p: (0, p[j])),
            ],
            out_specs=[pl.BlockSpec((tokens, step), lambda j, p: (0, j))]
            + [pl.BlockSpec((tokens, len(units) * unit), lambda j, p: (0, 0)) for units in sent],
        ),
        out_shape=[pltpu.HBM((tokens, width), F32)] + [pltpu.HBM((tokens, len(units) * unit), BF16) for units in sent],
        compiler_params=pltpu.CompilerParams(vmem_limit_bytes=VMEM),
        cost_estimate=CHEAP,
        name="act_parts",
    )(jnp.stack(columns).astype(jnp.int32), *pinned(acts, basis_in))


def grad_kernel(end_cuts, mid_cuts, outs, place_ref, basis_ref, *refs):
    refs, total_ref, out_refs = refs[: -outs - 1], refs[-outs - 1], refs[-outs:]

    def add(cuts):
        acc = total_ref[...]
        row = 0
        for n, first, width in cuts:
            piece = refs[n][:, first : first + width]
            acc = acc + jnp.dot(piece, basis_ref[row : row + width], preferred_element_type=F32)
            row += width
        if outs == 1:
            out_refs[0][...] = acc
            return
        for n, out_ref in enumerate(out_refs):

            @pl.when(pl.program_id(0) == n)
            def _(out_ref=out_ref):
                out_ref[...] = acc

    pl.when(place_ref[0] == 1)(lambda: add(end_cuts))
    pl.when(place_ref[0] == 0)(lambda: add(mid_cuts))


def grad_pieces(end, at_end, at_mid, place, basis_out, total, halves=False):
    arrays = []
    cuts = []
    for sources in (at_end, at_mid):
        cuts.append([])
        for array, first, width in sources:
            known = [n for n, other in enumerate(arrays) if other is array]
            if not known:
                arrays.append(array)
            cuts[-1].append((known[0] if known else len(arrays) - 1, first, width))
    depth = sum(width for _, _, width in cuts[0])
    tokens, width = total.shape
    step = width // 2
    out_spec = pl.BlockSpec((tokens, step), lambda j, s: (0, j))
    half_spec = pl.BlockSpec((tokens, step), lambda j, s: (0, 0))
    return pl.pallas_call(
        functools.partial(grad_kernel, *cuts, 2 if halves else 1),
        grid_spec=pltpu.PrefetchScalarGridSpec(
            num_scalar_prefetch=1,
            grid=(2,),
            in_specs=[pl.BlockSpec((depth, step), lambda j, s: (s[1], j))]
            + [pl.BlockSpec(array.shape, lambda j, s: (0, 0)) for array in arrays]
            + [out_spec],
            out_specs=[half_spec] * 2 if halves else out_spec,
        ),
        out_shape=[pltpu.HBM((tokens, step), F32)] * 2 if halves else pltpu.HBM((tokens, width), F32),
        compiler_params=pltpu.CompilerParams(vmem_limit_bytes=VMEM),
        cost_estimate=CHEAP,
        name="grad_pieces",
    )(jnp.stack([end.astype(jnp.int32), place.astype(jnp.int32)]), *pinned(basis_out), *arrays, *pinned(total))


def grad_sum_kernel(has_total, place_ref, *refs):
    out_ref, refs = refs[-1], refs[:-1]
    acc = None
    if has_total:
        acc, refs = refs[-1][...], refs[:-1]
    count = len(refs) // 2
    for block, basis in zip(refs[:count], refs[count:]):
        part = jnp.dot(block[...], basis[...], preferred_element_type=F32)
        acc = part if acc is None else acc + part
    out_ref[...] = acc


def grad_blocks(pieces, places, basis_out, total):
    tokens, depth = pieces[0].shape
    width = basis_out.shape[1]
    step = width // 2 if len(pieces) == 1 else 256
    whole = pl.BlockSpec((tokens, depth), lambda j, s: (0, 0))
    out_spec = pl.BlockSpec((tokens, step), lambda j, s: (0, j))

    def rows_of(n):
        return pl.BlockSpec((depth, step), lambda j, s: (s[n], j))

    totals = [] if total is None else [total]
    return pl.pallas_call(
        functools.partial(grad_sum_kernel, total is not None),
        grid_spec=pltpu.PrefetchScalarGridSpec(
            num_scalar_prefetch=1,
            grid=(width // step,),
            in_specs=[whole] * len(pieces) + [rows_of(n) for n in range(len(pieces))] + [out_spec] * len(totals),
            out_specs=out_spec,
        ),
        out_shape=pltpu.HBM((tokens, width), F32),
        compiler_params=pltpu.CompilerParams(vmem_limit_bytes=VMEM),
        cost_estimate=CHEAP,
        name="grad_blocks",
    )(jnp.stack(places).astype(jnp.int32), *pinned(*pieces, *[basis_out] * len(pieces), *totals))


def make_kernel(plans, place_ref, *refs):
    out_ref = refs[-1]

    def write(layers):
        at = 0
        for columns in layers:
            total = None
            for n, first, width in columns:
                block = refs[n][:, first : first + width]
                if len(columns) > 1:
                    block = block.astype(F32)
                total = block if total is None else total + block
            out_ref[:, at : at + columns[0][2]] = total.astype(out_ref.dtype)
            at += columns[0][2]

    for flag, layers in plans:
        if layers is not None:
            pl.when(place_ref[0] == flag)(lambda layers=layers: write(layers))


def make(end, at_end, at_mid, units, unit):
    arrays, specs, keys, plans = [], [], [], []
    small = units <= 2
    rows = (at_mid or at_end)[0][0][0].shape[0]
    steps = 1 if small else 2
    rows //= steps
    for flag, ranges in ((1, at_end), (0, at_mid)):
        if ranges is None:
            plans.append((flag, None))
            continue
        plan = []
        for sources in ranges:
            columns = []
            for array, first, count in sources:
                aligned = first % count == 0
                width = count * unit if aligned else array.shape[1]
                column = first // count if aligned else 0
                key = (id(array), width, column, flag)
                if key not in keys:
                    keys.append(key)
                    arrays.append(array)
                    specs.append(
                        pl.BlockSpec(
                            (rows, width),
                            lambda i, p, flag=flag, column=column: (i * (p[0] if flag else 1 - p[0]), column),
                        )
                    )
                columns.append((keys.index(key), 0 if aligned else first * unit, count * unit))
            plan.append(columns)
        plans.append((flag, plan))
    return pl.pallas_call(
        functools.partial(make_kernel, plans),
        grid_spec=pltpu.PrefetchScalarGridSpec(
            num_scalar_prefetch=1,
            grid=(steps,),
            in_specs=specs,
            out_specs=pl.BlockSpec((rows, units * unit), lambda i, p: (i, 0)),
        ),
        out_shape=(jax.ShapeDtypeStruct if small else pltpu.HBM)((steps * rows, units * unit), BF16),
        compiler_params=pltpu.CompilerParams(vmem_limit_bytes=VMEM),
        cost_estimate=CHEAP,
        name="make",
    )(end.astype(jnp.int32).reshape(1), *[a if a.shape[1] <= 2 * unit else pinned(a)[0] for a in arrays])


def tile_kernel(tokens, count, place_ref, low_ref, high_ref, *refs):
    out_ref = refs[-1]
    rows = low_ref.shape[1]
    for n in range(count):

        @pl.when(pl.program_id(0) == n)
        def _(n=n):
            for at, grad_ref in ((0, low_ref), (rows, high_ref)):
                tile = lax.dot_general(grad_ref[...], refs[n][...], TN, preferred_element_type=F32)
                out_ref[at : at + rows] = tile * tile / F32(tokens)


def tile_part(rot_grad, acts, columns, out, shape):
    tokens, rows = rot_grad[0].shape
    count = len(acts)
    width = acts[0].shape[1]
    outs = [] if out is None else [out]
    return pl.pallas_call(
        functools.partial(tile_kernel, tokens, count),
        grid_spec=pltpu.PrefetchScalarGridSpec(
            num_scalar_prefetch=1,
            grid=(count,),
            in_specs=[pl.BlockSpec((tokens, rows), lambda j, p: (0, 0))] * 2
            + [pl.BlockSpec((tokens, width), lambda j, p: (0, 0))] * count
            + [pl.BlockSpec(memory_space=pl.ANY)] * len(outs),
            out_specs=pl.BlockSpec((2 * rows, width), lambda j, p: (0, p[j])),
        ),
        out_shape=jax.ShapeDtypeStruct(shape, F32),
        input_output_aliases={3 + count: 0} if outs else {},
        compiler_params=pltpu.CompilerParams(vmem_limit_bytes=VMEM),
        cost_estimate=CHEAP,
        name="tile_part",
    )(jnp.stack(columns).astype(jnp.int32), *rot_grad, *acts, *outs)


def barrier(*values):
    return lax.optimization_barrier(values)


def grid_of_eight(grads, basis_out, acts, basis_in):
    o = lax.axis_index("out")
    z, x = o // 2, o % 2
    side = z // 2
    end = (z == 0) | (z == 3)
    near, far, farthest = z ^ 1, 2 - side, 3 - 3 * side
    eighth = basis_in.shape[1] // 8
    half = grads.shape[1] // 2

    def either(at_end, at_mid):
        return jnp.where(end, at_end, at_mid)

    def z_block(zb, xb):
        return zb * 2 + xb

    def column(ds, dx, h):
        return ((side ^ ds) * 2 + (x ^ dx)) * 2 + h

    unit = eighth // 2

    def blocks(pieces, places, total):
        return grad_blocks(pieces, places, basis_out, total)

    def block_of(at_end, at_mid, place, total, halves=False):
        at_end = [(array, first * unit, units * unit) for array, first, units in at_end]
        at_mid = [(array, first * unit, units * unit) for array, first, units in at_mid]
        return grad_pieces(end, at_end, at_mid, place, basis_out, total, halves)

    def put(at_end, at_mid, units):
        return make(end, at_end, at_mid, units, unit)

    def one(array, first, units):
        return [[(array, first, units)]]

    a = send("near", grads, Z_NEAR)
    x0 = send("own_x", grads, X_ALL)
    b1 = send("mid_own", grads, Z_MID)
    order = [(1, 1, 0), (1, 0, 0), (0, 1, 0), (0, 0, 0), (1, 1, 1), (1, 0, 1), (0, 1, 1), (0, 0, 1)]
    sent = [0, 1, 2, 3, 4, 5, 6], [8, 9, 10, 11, 7], [12, 13, 14, 15]
    wide, n1, n2, n3 = act_parts([column(*e) for e in order], sent, unit, acts, basis_in)
    total = blocks([after(grads, wide)], [z_block(z, x)], None)

    a, total = barrier(a, total)
    c1 = send("near_on", a, X_END_Z_MID)
    b1, total = barrier(b1, total)
    y1 = put(one(n1, 0, 7), one(b1, 0, 7), 7)
    r1 = send("r1", y1, Z_NEAR)
    xb1 = send("mid_own_x", after(b1, y1), X_MID)
    total = blocks([a, x0], [z_block(near, x), z_block(z, 1 - x)], total)

    b2, total = barrier(c1, total)
    y2 = put(one(n2, 0, 5), one(b2, 0, 5), 5)
    r2_h = send("r2_h", y2, Z_NEAR)
    r1, y2, total = barrier(r1, y2, total)
    y3 = put(one(r1, 0, 7), one(b2, 0, 7), 7)
    x2 = send("x2", y3, X_ALL)
    y4 = put(None, [[(after(wide, y3), 0, 4), (r1, 0, 4)]], 4)
    m_a = send("mid_a", y4, Z_MID)
    y5 = put(one(after(n3, y4), 0, 4), one(b2, 5, 2), 4)
    r2_t = send("r2_t", y5, Z_NEAR)
    xb1, total = barrier(xb1, total)
    total = block_of([(b2, 0, 7)], [(xb1, 0, 7)], z_block(either(near, far), 1 - x), after(total, y5))
    total = block_of([(r1, 0, 7)], [(b1, 0, 7)], z_block(far, x), total)

    r2_h, total = barrier(r2_h, total)
    y6 = put(None, [[(wide, 8, 4), (r2_h, 0, 4)]], 4)
    m_b = send("mid_b", y6, Z_MID)
    x3_h = send("x3_h", after(r2_h, y6), X_END)
    m_a, y6, total = barrier(m_a, y6, total)
    y7 = put(None, [[(wide, 4, 2), (r1, 4, 2), (m_a, 0, 2)]], 2)
    xm_a = send("sum_x_a", y7, X_MID)
    x2, total = barrier(x2, after(total, y7))
    total = blocks([x2], [z_block(either(far, farthest), 1 - x)], total)

    r2_t, total = barrier(r2_t, total)
    xm_a, total = barrier(xm_a, total)
    sums = [
        [(r1, 6, 1), (wide, 6, 1), (m_a, 2, 1), (xm_a, 0, 1)],
        [(r2_h, 4, 1), (wide, 7, 1), (m_a, 3, 1), (xm_a, 1, 1)],
    ]
    t00_a = put(one(x0, 2, 2), sums, 2)
    e00_a = send("all_in_0a", t00_a, Z_NEAR)
    t10_a = send("all_mid_a", t00_a, Z_MID)
    m_b, t00_a = barrier(m_b, t00_a)
    y9 = put(None, [[(after(wide, t00_a), 12, 2), (r2_t, 0, 2), (m_b, 0, 2)]], 2)
    xm_b = send("sum_x_b", y9, X_MID)
    y8 = put(one(after(r2_t, y9), 0, 2), one(a, 0, 2), 2)

    e00_a, y8 = barrier(e00_a, y8)
    t10_a, y8 = barrier(t10_a, y8)
    y10 = put(one(x0, 4, 2), one(t10_a, 0, 2), 2)
    e10_a = send("all_in_1a", y10, Z_NEAR)
    x3_h, y10 = barrier(x3_h, y10)
    x3_t = send("x3_t", after(y8, y10), X_ALL)
    xm_b, y10 = barrier(xm_b, y10)
    sums = [[(after(wide, y10), 14, 2), (r2_t, 2, 2), (m_b, 2, 2), (xm_b, 0, 2)]]
    t00_b = put(one(x0, 6, 1), sums, 2)
    e00_b = send("all_in_0b", t00_b, Z_NEAR)
    t10_b = send("all_mid_b", t00_b, Z_MID)
    u00_a = put(one(after(e00_a, t00_b), 0, 2), one(t00_a, 0, 2), 2)
    s01_a = send("all_x_0a", u00_a, X_ALL)

    e10_a, u00_a = barrier(e10_a, u00_a)
    u10_a = put(one(e10_a, 0, 2), one(after(t10_a, u00_a), 0, 2), 2)
    s11_a = send("all_x_1a", u10_a, X_ALL)
    total = block_of([(r2_h, 0, 5), (r2_t, 0, 2)], [(b2, 0, 7)], z_block(farthest, x), after(total, u10_a))
    x3_t, total = barrier(x3_t, total)

    e00_b, total = barrier(e00_b, total)
    t10_b, total = barrier(t10_b, total)
    e10_b = send("all_in_1b", t10_b, Z_IN)
    u00_b = put(one(e00_b, 0, 2), one(t00_b, 0, 2), 2)
    s01_b = send("all_x_0b", u00_b, X_ALL)
    s01_a, total = barrier(s01_a, after(total, u00_b))
    at_end = [(x3_h, 0, 5), (x3_t, 0, 2)]
    at_mid = [(x3_t, 0, 2), (e00_a, 0, 2), (e10_a, 0, 2), (e00_b, 0, 1)]
    low, high = block_of(at_end, at_mid, z_block(either(farthest, near), 1 - x), total, halves=True)

    s11_a, e10_b, low, high = barrier(s11_a, e10_b, low, high)
    low_other = send("core_low", low, [(0, 1), (1, 0)], "inp")
    high_other = send("core_high", high, [(0, 1), (1, 0)], "inp")
    u10_b = put(one(e10_b, 0, 2), one(t10_b, 0, 2), 2)
    s11_b = send("all_x_1b", u10_b, X_ALL)
    rot_grad = [
        (mine + theirs).astype(BF16) for mine, theirs in ((after(low, u10_b), low_other), (after(high, u10_b), high_other))
    ]
    shape = (basis_out.shape[1], basis_in.shape[1])
    places = [column(0, 0, 0), column(1, 0, 0), column(0, 1, 0), column(1, 1, 0)]
    out = tile_part(rot_grad, [u00_a, u10_a, s01_a, s11_a], places, None, shape)
    s01_b, out = barrier(s01_b, out)
    out = tile_part(rot_grad, [u00_b, u10_b, s01_b], [column(0, 0, 1), column(1, 0, 1), column(0, 1, 1)], out, shape)
    return tile_part(rot_grad, [s11_b], [column(1, 1, 1)], out, shape)


def solution(mesh):
    return jax.shard_map(
        grid_of_eight if mesh.shape["out"] == 8 and mesh.shape["inp"] == 2 else plain,
        mesh=mesh,
        in_specs=(
            P("groups", ("inp", "out")),
            P("inp", "out"),
            P("groups", "out"),
            P("out", "inp"),
        ),
        out_specs=P(("groups", "out"), "inp"),
        check_vma=False,
    )
```

```python
import functools

import jax
import jax.numpy as jnp
from jax import lax
from jax.experimental import pallas as pl
from jax.experimental.pallas import tpu as pltpu
from jax.sharding import PartitionSpec as P

F32, BF16 = jnp.float32, jnp.bfloat16
TN = (((0,), (0,)), ((), ()))
VMEM = 44 * 1024 * 1024
CHEAP = pl.CostEstimate(flops=1000, bytes_accessed=1000, transcendentals=0)


def plain(grads, basis_out, acts, basis_in):
    partial_grad = jnp.dot(
        lax.all_gather(grads, "out", axis=1, tiled=True),
        basis_out,
        preferred_element_type=F32,
    )
    rot_grad = lax.psum(partial_grad, "inp").astype(BF16)
    contract = (((0,), (1,)), ((), ()))
    act_full = lax.dot_general(basis_in, acts, contract, preferred_element_type=F32)
    rot_act = lax.psum(act_full, "out").astype(BF16)
    tile = lax.dot_general(rot_grad, rot_act, contract, preferred_element_type=F32)
    return tile * tile / F32(rot_grad.shape[0])


def pairs(fn):
    out = []
    for z in range(4):
        for x in range(2):
            to = fn(z, x)
            if to is not None:
                out.append((z * 2 + x, to[0] * 2 + to[1]))
    return out


def is_end(z):
    return z in (0, 3)


X_ALL = pairs(lambda z, x: (z, 1 - x))
X_END = pairs(lambda z, x: (z, 1 - x) if is_end(z) else None)
X_MID = pairs(lambda z, x: None if is_end(z) else (z, 1 - x))
Z_NEAR = pairs(lambda z, x: (z ^ 1, x))
Z_MID = pairs(lambda z, x: None if is_end(z) else (3 - z, x))
X_END_Z_MID = pairs(lambda z, x: (z, 1 - x) if is_end(z) else (3 - z, x))
Z_IN = pairs(lambda z, x: None if is_end(z) else (z ^ 1, x))


def send(name, value, way, axis="out", full=False):
    if full:
        axis = ("groups", "out")
        idle = [n for n in range(8) if n not in [source for source, _ in way]]
        way = [(g * 8 + a, g * 8 + b) for g in range(2) for a, b in way]
        way += [(g * 8 + n, (1 - g) * 8 + n) for g in range(2) for n in idle]
    with jax.named_scope(name):
        return lax.ppermute(value, axis, way)


def after(value, *events):
    return lax.optimization_barrier((value, *events))[0]


def pinned(*arrays):
    return [pltpu.with_memory_space_constraint(array, pltpu.HBM) for array in arrays]


def act_kernel(spans, place_ref, acts_ref, basis_ref, wide_ref, *narrow_refs):
    part = jnp.dot(acts_ref[...], basis_ref[...], preferred_element_type=F32)
    wide_ref[...] = part
    narrow = part.astype(BF16)
    for j, pieces in enumerate(spans):

        @pl.when(pl.program_id(0) == j)
        def _(pieces=pieces):
            for n, into, first, width in pieces:
                narrow_refs[n][:, into : into + width] = narrow[:, first : first + width]


def act_parts(columns, sent, unit, acts, basis_in):
    tokens, depth = acts.shape
    width = basis_in.shape[1]
    step = 2 * unit
    spans = [[] for _ in columns]
    for n, units in enumerate(sent):
        for at, u in enumerate(units):
            spans[u // 2].append((n, at * unit, (u % 2) * unit, unit))
    return pl.pallas_call(
        functools.partial(act_kernel, spans),
        grid_spec=pltpu.PrefetchScalarGridSpec(
            num_scalar_prefetch=1,
            grid=(len(columns),),
            in_specs=[
                pl.BlockSpec((tokens, depth), lambda j, p: (0, 0)),
                pl.BlockSpec((depth, step), lambda j, p: (0, p[j])),
            ],
            out_specs=[pl.BlockSpec((tokens, step), lambda j, p: (0, j))]
            + [pl.BlockSpec((tokens, len(units) * unit), lambda j, p: (0, 0)) for units in sent],
        ),
        out_shape=[pltpu.HBM((tokens, width), F32)] + [pltpu.HBM((tokens, len(units) * unit), BF16) for units in sent],
        compiler_params=pltpu.CompilerParams(vmem_limit_bytes=VMEM),
        cost_estimate=CHEAP,
        name="act_parts",
    )(jnp.stack(columns).astype(jnp.int32), *pinned(acts, basis_in))


def grad_kernel(end_cuts, mid_cuts, outs, place_ref, basis_ref, *refs):
    refs, total_ref, out_refs = refs[: -outs - 1], refs[-outs - 1], refs[-outs:]

    def add(cuts):
        acc = total_ref[...]
        row = 0
        for n, first, width in cuts:
            piece = refs[n][:, first : first + width]
            acc = acc + jnp.dot(piece, basis_ref[row : row + width], preferred_element_type=F32)
            row += width
        if outs == 1:
            out_refs[0][...] = acc
            return
        for n, out_ref in enumerate(out_refs):

            @pl.when(pl.program_id(0) == n)
            def _(out_ref=out_ref):
                out_ref[...] = acc

    pl.when(place_ref[0] == 1)(lambda: add(end_cuts))
    pl.when(place_ref[0] == 0)(lambda: add(mid_cuts))


def grad_pieces(end, at_end, at_mid, place, basis_out, total, halves=False):
    arrays = []
    cuts = []
    for sources in (at_end, at_mid):
        cuts.append([])
        for array, first, width in sources:
            known = [n for n, other in enumerate(arrays) if other is array]
            if not known:
                arrays.append(array)
            cuts[-1].append((known[0] if known else len(arrays) - 1, first, width))
    depth = sum(width for _, _, width in cuts[0])
    tokens, width = total.shape
    step = width // 2
    out_spec = pl.BlockSpec((tokens, step), lambda j, s: (0, j))
    half_spec = pl.BlockSpec((tokens, step), lambda j, s: (0, 0))
    return pl.pallas_call(
        functools.partial(grad_kernel, *cuts, 2 if halves else 1),
        grid_spec=pltpu.PrefetchScalarGridSpec(
            num_scalar_prefetch=1,
            grid=(2,),
            in_specs=[pl.BlockSpec((depth, step), lambda j, s: (s[1], j))]
            + [pl.BlockSpec(array.shape, lambda j, s: (0, 0)) for array in arrays]
            + [out_spec],
            out_specs=[half_spec] * 2 if halves else out_spec,
        ),
        out_shape=[pltpu.HBM((tokens, step), F32)] * 2 if halves else pltpu.HBM((tokens, width), F32),
        compiler_params=pltpu.CompilerParams(vmem_limit_bytes=VMEM),
        cost_estimate=CHEAP,
        name="grad_pieces",
    )(jnp.stack([end.astype(jnp.int32), place.astype(jnp.int32)]), *pinned(basis_out), *arrays, *pinned(total))


def grad_sum_kernel(has_total, place_ref, *refs):
    out_ref, refs = refs[-1], refs[:-1]
    acc = None
    if has_total:
        acc, refs = refs[-1][...], refs[:-1]
    count = len(refs) // 2
    for block, basis in zip(refs[:count], refs[count:]):
        part = jnp.dot(block[...], basis[...], preferred_element_type=F32)
        acc = part if acc is None else acc + part
    out_ref[...] = acc


def grad_blocks(pieces, places, basis_out, total):
    tokens, depth = pieces[0].shape
    width = basis_out.shape[1]
    step = width // 2 if len(pieces) == 1 else 256
    whole = pl.BlockSpec((tokens, depth), lambda j, s: (0, 0))
    out_spec = pl.BlockSpec((tokens, step), lambda j, s: (0, j))

    def rows_of(n):
        return pl.BlockSpec((depth, step), lambda j, s: (s[n], j))

    totals = [] if total is None else [total]
    return pl.pallas_call(
        functools.partial(grad_sum_kernel, total is not None),
        grid_spec=pltpu.PrefetchScalarGridSpec(
            num_scalar_prefetch=1,
            grid=(width // step,),
            in_specs=[whole] * len(pieces) + [rows_of(n) for n in range(len(pieces))] + [out_spec] * len(totals),
            out_specs=out_spec,
        ),
        out_shape=pltpu.HBM((tokens, width), F32),
        compiler_params=pltpu.CompilerParams(vmem_limit_bytes=VMEM),
        cost_estimate=CHEAP,
        name="grad_blocks",
    )(jnp.stack(places).astype(jnp.int32), *pinned(*pieces, *[basis_out] * len(pieces), *totals))


def make_kernel(plans, place_ref, *refs):
    out_ref = refs[-1]

    def write(layers):
        at = 0
        for columns in layers:
            total = None
            for n, first, width in columns:
                block = refs[n][:, first : first + width]
                if len(columns) > 1:
                    block = block.astype(F32)
                total = block if total is None else total + block
            out_ref[:, at : at + columns[0][2]] = total.astype(out_ref.dtype)
            at += columns[0][2]

    for flag, layers in plans:
        if layers is not None:
            pl.when(place_ref[0] == flag)(lambda layers=layers: write(layers))


def make(end, at_end, at_mid, units, unit):
    arrays, specs, keys, plans = [], [], [], []
    small = units <= 2
    rows = (at_mid or at_end)[0][0][0].shape[0]
    steps = 1 if small else 2
    rows //= steps
    for flag, ranges in ((1, at_end), (0, at_mid)):
        if ranges is None:
            plans.append((flag, None))
            continue
        plan = []
        for sources in ranges:
            columns = []
            for array, first, count in sources:
                aligned = first % count == 0
                width = count * unit if aligned else array.shape[1]
                column = first // count if aligned else 0
                key = (id(array), width, column, flag)
                if key not in keys:
                    keys.append(key)
                    arrays.append(array)
                    specs.append(
                        pl.BlockSpec(
                            (rows, width),
                            lambda i, p, flag=flag, column=column: (i * (p[0] if flag else 1 - p[0]), column),
                        )
                    )
                columns.append((keys.index(key), 0 if aligned else first * unit, count * unit))
            plan.append(columns)
        plans.append((flag, plan))
    return pl.pallas_call(
        functools.partial(make_kernel, plans),
        grid_spec=pltpu.PrefetchScalarGridSpec(
            num_scalar_prefetch=1,
            grid=(steps,),
            in_specs=specs,
            out_specs=pl.BlockSpec((rows, units * unit), lambda i, p: (i, 0)),
        ),
        out_shape=(jax.ShapeDtypeStruct if small else pltpu.HBM)((steps * rows, units * unit), BF16),
        compiler_params=pltpu.CompilerParams(vmem_limit_bytes=VMEM),
        cost_estimate=CHEAP,
        name="make",
    )(end.astype(jnp.int32).reshape(1), *[a if a.shape[1] <= 2 * unit else pinned(a)[0] for a in arrays])


def tile_kernel(tokens, count, place_ref, low_ref, high_ref, *refs):
    out_ref = refs[-1]
    rows = low_ref.shape[1]
    for n in range(count):

        @pl.when(pl.program_id(0) == n)
        def _(n=n):
            for at, grad_ref in ((0, low_ref), (rows, high_ref)):
                tile = lax.dot_general(grad_ref[...], refs[n][...], TN, preferred_element_type=F32)
                out_ref[at : at + rows] = tile * tile / F32(tokens)


def tile_part(rot_grad, acts, columns, out, shape):
    tokens, rows = rot_grad[0].shape
    count = len(acts)
    width = acts[0].shape[1]
    outs = [] if out is None else [out]
    return pl.pallas_call(
        functools.partial(tile_kernel, tokens, count),
        grid_spec=pltpu.PrefetchScalarGridSpec(
            num_scalar_prefetch=1,
            grid=(count,),
            in_specs=[pl.BlockSpec((tokens, rows), lambda j, p: (0, 0))] * 2
            + [pl.BlockSpec((tokens, width), lambda j, p: (0, 0))] * count
            + [pl.BlockSpec(memory_space=pl.ANY)] * len(outs),
            out_specs=pl.BlockSpec((2 * rows, width), lambda j, p: (0, p[j])),
        ),
        out_shape=jax.ShapeDtypeStruct(shape, F32),
        input_output_aliases={3 + count: 0} if outs else {},
        compiler_params=pltpu.CompilerParams(vmem_limit_bytes=VMEM),
        cost_estimate=CHEAP,
        name="tile_part",
    )(jnp.stack(columns).astype(jnp.int32), *rot_grad, *acts, *outs)


def barrier(*values):
    return lax.optimization_barrier(values)


def grid_of_eight(grads, basis_out, acts, basis_in):
    o = lax.axis_index("out")
    z, x = o // 2, o % 2
    side = z // 2
    end = (z == 0) | (z == 3)
    near, far, farthest = z ^ 1, 2 - side, 3 - 3 * side
    eighth = basis_in.shape[1] // 8
    half = grads.shape[1] // 2

    def either(at_end, at_mid):
        return jnp.where(end, at_end, at_mid)

    def z_block(zb, xb):
        return zb * 2 + xb

    def column(ds, dx, h):
        return ((side ^ ds) * 2 + (x ^ dx)) * 2 + h

    unit = eighth // 2

    def blocks(pieces, places, total):
        return grad_blocks(pieces, places, basis_out, total)

    def block_of(at_end, at_mid, place, total, halves=False):
        at_end = [(array, first * unit, units * unit) for array, first, units in at_end]
        at_mid = [(array, first * unit, units * unit) for array, first, units in at_mid]
        return grad_pieces(end, at_end, at_mid, place, basis_out, total, halves)

    def put(at_end, at_mid, units):
        return make(end, at_end, at_mid, units, unit)

    def one(array, first, units):
        return [[(array, first, units)]]

    a = send("near", grads, Z_NEAR)
    x0 = send("own_x", grads, X_ALL)
    b1 = send("mid_own", grads, Z_MID, full=True)
    order = [(1, 1, 0), (1, 0, 0), (0, 1, 0), (0, 0, 0), (1, 1, 1), (1, 0, 1), (0, 1, 1), (0, 0, 1)]
    sent = [0, 1, 2, 3, 4, 5, 6], [8, 9, 10, 11, 7], [12, 13, 14, 15]
    wide, n1, n2, n3 = act_parts([column(*e) for e in order], sent, unit, acts, basis_in)
    total = blocks([after(grads, wide)], [z_block(z, x)], None)

    a, total = barrier(a, total)
    c1 = send("near_on", a, X_END_Z_MID)
    b1, total = barrier(b1, total)
    y1 = put(one(n1, 0, 7), one(b1, 0, 7), 7)
    r1 = send("r1", y1, Z_NEAR)
    xb1 = send("mid_own_x", after(b1, y1), X_MID, full=True)
    total = blocks([a, x0], [z_block(near, x), z_block(z, 1 - x)], total)

    b2, total = barrier(c1, total)
    y2 = put(one(n2, 0, 5), one(b2, 0, 5), 5)
    r2_h = send("r2_h", y2, Z_NEAR)
    r1, y2, total = barrier(r1, y2, total)
    y3 = put(one(r1, 0, 7), one(b2, 0, 7), 7)
    x2 = send("x2", y3, X_ALL)
    y4 = put(None, [[(after(wide, y3), 0, 4), (r1, 0, 4)]], 4)
    m_a = send("mid_a", y4, Z_MID, full=True)
    y5 = put(one(after(n3, y4), 0, 4), one(b2, 5, 2), 4)
    r2_t = send("r2_t", y5, Z_NEAR)
    xb1, total = barrier(xb1, total)
    total = block_of([(b2, 0, 7)], [(xb1, 0, 7)], z_block(either(near, far), 1 - x), after(total, y5))
    total = block_of([(r1, 0, 7)], [(b1, 0, 7)], z_block(far, x), total)

    r2_h, total = barrier(r2_h, total)
    y6 = put(None, [[(wide, 8, 4), (r2_h, 0, 4)]], 4)
    m_b = send("mid_b", y6, Z_MID, full=True)
    x3_h = send("x3_h", after(r2_h, y6), X_END, full=True)
    m_a, y6, total = barrier(m_a, y6, total)
    y7 = put(None, [[(wide, 4, 2), (r1, 4, 2), (m_a, 0, 2)]], 2)
    xm_a = send("sum_x_a", y7, X_MID)
    x2, total = barrier(x2, after(total, y7))
    total = blocks([x2], [z_block(either(far, farthest), 1 - x)], total)

    r2_t, total = barrier(r2_t, total)
    xm_a, total = barrier(xm_a, total)
    sums = [
        [(r1, 6, 1), (wide, 6, 1), (m_a, 2, 1), (xm_a, 0, 1)],
        [(r2_h, 4, 1), (wide, 7, 1), (m_a, 3, 1), (xm_a, 1, 1)],
    ]
    t00_a = put(one(x0, 2, 2), sums, 2)
    e00_a = send("all_in_0a", t00_a, Z_NEAR)
    t10_a = send("all_mid_a", t00_a, Z_MID)
    m_b, t00_a = barrier(m_b, t00_a)
    y9 = put(None, [[(after(wide, t00_a), 12, 2), (r2_t, 0, 2), (m_b, 0, 2)]], 2)
    xm_b = send("sum_x_b", y9, X_MID)
    y8 = put(one(after(r2_t, y9), 0, 2), one(a, 0, 2), 2)

    e00_a, y8 = barrier(e00_a, y8)
    t10_a, y8 = barrier(t10_a, y8)
    y10 = put(one(x0, 4, 2), one(t10_a, 0, 2), 2)
    e10_a = send("all_in_1a", y10, Z_NEAR)
    x3_h, y10 = barrier(x3_h, y10)
    x3_t = send("x3_t", after(y8, y10), X_ALL)
    xm_b, y10 = barrier(xm_b, y10)
    sums = [[(after(wide, y10), 14, 2), (r2_t, 2, 2), (m_b, 2, 2), (xm_b, 0, 2)]]
    t00_b = put(one(x0, 6, 1), sums, 2)
    e00_b = send("all_in_0b", t00_b, Z_NEAR)
    t10_b = send("all_mid_b", t00_b, Z_MID)
    u00_a = put(one(after(e00_a, t00_b), 0, 2), one(t00_a, 0, 2), 2)
    s01_a = send("all_x_0a", u00_a, X_ALL)

    e10_a, u00_a = barrier(e10_a, u00_a)
    u10_a = put(one(e10_a, 0, 2), one(after(t10_a, u00_a), 0, 2), 2)
    s11_a = send("all_x_1a", u10_a, X_ALL)
    total = block_of([(r2_h, 0, 5), (r2_t, 0, 2)], [(b2, 0, 7)], z_block(farthest, x), after(total, u10_a))
    x3_t, total = barrier(x3_t, total)

    e00_b, total = barrier(e00_b, total)
    t10_b, total = barrier(t10_b, total)
    e10_b = send("all_in_1b", t10_b, Z_IN)
    u00_b = put(one(e00_b, 0, 2), one(t00_b, 0, 2), 2)
    s01_b = send("all_x_0b", u00_b, X_ALL)
    s01_a, total = barrier(s01_a, after(total, u00_b))
    at_end = [(x3_h, 0, 5), (x3_t, 0, 2)]
    at_mid = [(x3_t, 0, 2), (e00_a, 0, 2), (e10_a, 0, 2), (e00_b, 0, 1)]
    low, high = block_of(at_end, at_mid, z_block(either(farthest, near), 1 - x), total, halves=True)

    s11_a, e10_b, low, high = barrier(s11_a, e10_b, low, high)
    low_other = send("core_low", low, [(0, 1), (1, 0)], "inp")
    high_other = send("core_high", high, [(0, 1), (1, 0)], "inp")
    u10_b = put(one(e10_b, 0, 2), one(t10_b, 0, 2), 2)
    s11_b = send("all_x_1b", u10_b, X_ALL)
    rot_grad = [
        (mine + theirs).astype(BF16) for mine, theirs in ((after(low, u10_b), low_other), (after(high, u10_b), high_other))
    ]
    shape = (basis_out.shape[1], basis_in.shape[1])
    places = [column(0, 0, 0), column(1, 0, 0), column(0, 1, 0), column(1, 1, 0)]
    out = tile_part(rot_grad, [u00_a, u10_a, s01_a, s11_a], places, None, shape)
    s01_b, out = barrier(s01_b, out)
    out = tile_part(rot_grad, [u00_b, u10_b, s01_b], [column(0, 0, 1), column(1, 0, 1), column(0, 1, 1)], out, shape)
    return tile_part(rot_grad, [s11_b], [column(1, 1, 1)], out, shape)


def solution(mesh):
    return jax.shard_map(
        grid_of_eight if tuple(mesh.shape[n] for n in ("groups", "out", "inp")) == (2, 8, 2) else plain,
        mesh=mesh,
        in_specs=(
            P("groups", ("inp", "out")),
            P("inp", "out"),
            P("groups", "out"),
            P("out", "inp"),
        ),
        out_specs=P(("groups", "out"), "inp"),
        check_vma=False,
    )
```
